128 devices in a mesh: gx: 16 (over x, z), gy: 8 (over y, core).
Axes of the slice: x: 4, y: 4, z: 4, core: 2. Of those that a mesh axis runs over, the one named last changes fastest.
Arguments:
- source: float32 [128, 512, 256], P('gx', 'gy'), may hold values from -4.5 to 4.5
- cell_inverse: float32 [128, 512, 256], P('gx', 'gy'), may hold values from 0.8 to 1
- face_coefficients: float32 [6, 128, 512, 256], P(None, 'gx', 'gy'), may hold values from 0.02 to 0.75
- tile_counts: int32 [128, 128], P(('gx', 'gy')), may hold values from 0 to 32, as said below
- perf_cells: int32 [128, 128, 32], P(('gx', 'gy')), may hold values from 0 to 131071
- segment_kinds: int32 [524288], P(('gx', 'gy')), may hold values from 0 to 2, as said below
- segment_inverse: float32 [4, 4, 524288], P(None, None, ('gx', 'gy')), may hold values from -0.15 to 1
- upstream_coupling: float32 [4, 4, 524288], P(None, None, ('gx', 'gy')), may hold values from -0.45 to 0.07
- downstream_coupling: float32 [4, 4, 524288], P(None, None, ('gx', 'gy')), may hold values from -0.45 to 0.07
- perf_to_segment: float32 [4, 524288], P(None, ('gx', 'gy')), may hold values from -0.2 to 0.2
- segment_to_perf: float32 [4, 524288], P(None, ('gx', 'gy')), may hold values from -0.15 to 0.15
- segment_source: float32 [4, 524288], P(None, ('gx', 'gy')), may hold values from -6 to 6
Outputs:
- adjoint_cells: float32 [128, 512, 256], P('gx', 'gy')
- well_adjoint: float32 [4, 524288], P(None, ('gx', 'gy'))
The draws below stay inside these ranges and needn't reach their ends.
Inputs may be any that keep to these rules, and one draw needn't show every extreme that they name: Slot k of tile t toward owner o is used exactly when k < tile_counts[t, o], and segment o * 4096 + t * 32 + k is not empty exactly when its slot is used; the non-empty segments of one owner form one cyclic run of consecutive indices inside its block of 4096. `segment_kinds`: 0: an empty slot; 1: the last segment of its well; 2: a segment whose well continues at the next index of the same owner's block, cyclically.
All inputs are finite; a program needn't handle non-finite values.
Results may differ from the reference program's by a relative error of at most 0.00013.
Values sent between devices are 32-bit elements; how exact they have to be, the bound alone decides.
No kernel may reach another device: no remote copies, remote signals or barrier semaphores. Data moves between devices by JAX's collectives and lax.ppermute only.
A program may use at most 128 MiB of HBM per device.

```python
import jax
import jax.numpy as jnp
from jax import lax

CX = 8
CY = 64
NZ = 256
SEG_DEV = 4096
SEG_VARS = 4
ITERS = 8
WELL_MEAN = 300
NX = 128
NY = 512
CAP = 32
TOTAL_SEGS = 524288
N_GX = 16
N_GY = 8
DEVICES = 128


def owner_layout(key):
    subkey = jax.random.fold_in(key, 7)
    offset_key, level_key, full_key, end_key = jax.random.split(subkey, 4)
    owners = jnp.arange(DEVICES, dtype=jnp.int32)
    offsets = jax.random.randint(offset_key, (DEVICES,), 0, DEVICES)
    levels = jax.random.randint(level_key, (DEVICES,), 0, 4)
    full_owner = jax.random.randint(full_key, (), 0, DEVICES)
    levels = jnp.where(owners == full_owner, 0, levels)
    active = jnp.right_shift(jnp.full((DEVICES,), SEG_DEV, jnp.int32), levels)
    tile_index = jnp.arange(DEVICES, dtype=jnp.int32)
    run_start = jnp.mod(tile_index[:, None] - offsets[None, :], DEVICES) * CAP
    counts = jnp.clip(active[None, :] - run_start, 0, CAP)
    slot_index = jnp.arange(CAP, dtype=jnp.int32)
    run_rank = run_start.T[:, :, None] + slot_index[None, None, :]
    well_ends = jax.random.randint(end_key, (DEVICES, DEVICES, CAP), 0, WELL_MEAN) == 0
    final_slot = run_rank == active[:, None, None] - 1
    segment_kinds = jnp.where(run_rank >= active[:, None, None], 0, jnp.where(final_slot | well_ends, 1, 2))
    return (counts.astype(jnp.int32), segment_kinds.reshape(DEVICES * SEG_DEV).astype(jnp.int32))


def dominant_blocks(key, low, high, spread):
    spread_key, diagonal_key = jax.random.split(key)
    off_diagonal = jax.random.uniform(spread_key, (SEG_VARS, SEG_VARS, TOTAL_SEGS), jnp.float32, -spread, spread)
    diagonal = jax.random.uniform(diagonal_key, (SEG_VARS, 1, TOTAL_SEGS), jnp.float32, low, high)
    identity = (jnp.arange(SEG_VARS)[:, None] == jnp.arange(SEG_VARS)[None, :])[:, :, None]
    return jnp.where(identity, diagonal, off_diagonal)


def draw_tile_counts(key, part):
    return owner_layout(key)[0]


def draw_segment_kinds(key, part):
    return owner_layout(key)[1]


def draw_source(key, part):
    key = jax.random.fold_in(key, 3)
    return jnp.clip(jax.random.normal(key, (NX, NY, NZ), jnp.float32), -4.5, 4.5)


def draw_face_coefficients(key, part):
    key = jax.random.fold_in(key, 5)
    unit_draw = jax.random.uniform(key, (6, NX, NY, NZ), jnp.float32)
    strong = (jnp.arange(6) == 0)[:, None, None, None]
    return jnp.where(strong, 0.35 + 0.4 * unit_draw, 0.02 + 0.03 * unit_draw)


def draw_segment_inverse(key, part):
    key = jax.random.fold_in(key, 9)
    return dominant_blocks(key, 0.7, 1.0, 0.15)


def draw_upstream_coupling(key, part):
    key = jax.random.fold_in(key, 11)
    return dominant_blocks(key, -0.42, -0.28, 0.07)


def draw_downstream_coupling(key, part):
    key = jax.random.fold_in(key, 13)
    return dominant_blocks(key, -0.42, -0.28, 0.07)


def plant(result, own_key, low, high):
    place = [jax.random.randint(jax.random.fold_in(own_key, axis), (), 0, length) for axis, length in enumerate(result.shape)]
    widest = result.shape.index(max(result.shape))
    next_to = place[:widest] + [(place[widest] + 1) % result.shape[widest]] + place[widest + 1:]
    return result.at[tuple(place)].set(low).at[tuple(next_to)].set(high)


def steps_of(key, shape, cuts, smallest, top_value):
    def one(position, blocks):
        heights = jax.random.uniform(jax.random.fold_in(jax.random.fold_in(key, 6), position), (blocks,), jnp.float32, smallest / len(cuts), top_value / len(cuts))
        return jnp.repeat(jnp.exp(heights), shape[position] // blocks).reshape((-1,) + (1,) * (len(shape) - position - 1))

    loudness = one(*cuts[0])
    for cut in cuts[1:]:
        loudness = loudness * one(*cut)
    return loudness


def scatter_about(key, shape, deviation, bound, pieces=(), kind=jnp.bfloat16):
    level = steps_of(key, shape, pieces, -0.22, 0.18) if pieces else 1.0
    entries = jax.random.normal(key, shape, jnp.float32) * deviation * level
    return jnp.minimum(jnp.maximum(entries, -bound), bound).astype(kind)


def setup_inputs(seed: int = 0) -> dict:
    splits = jax.random.split(jax.random.key(seed), 13)
    return {
        "source": draw_source(jax.random.fold_in(splits[12], 71), 0),
        "cell_inverse": jnp.clip(0.8 + 0.19999999 * jax.random.uniform(splits[1], (NX, NY, NZ), jnp.float32) ** steps_of(splits[1], (NX, NY, NZ), ((0, 16), (1, 8)), -0.2, 0.2), 0.8, 1.0),
        "face_coefficients": draw_face_coefficients(jax.random.fold_in(splits[12], 71), 0),
        "tile_counts": draw_tile_counts(jax.random.fold_in(splits[12], 71), 0),
        "perf_cells": plant(jax.random.randint(splits[4], (DEVICES, DEVICES, CAP), 0, CX * CY * NZ), jax.random.fold_in(splits[4], 1), 0, (CX * CY * NZ) - 1).astype(jnp.int32),
        "segment_kinds": draw_segment_kinds(jax.random.fold_in(splits[12], 71), 0),
        "segment_inverse": draw_segment_inverse(jax.random.fold_in(splits[12], 71), 0),
        "upstream_coupling": draw_upstream_coupling(jax.random.fold_in(splits[12], 71), 0),
        "downstream_coupling": draw_downstream_coupling(jax.random.fold_in(splits[12], 71), 0),
        "perf_to_segment": jnp.clip(jax.random.uniform(splits[9], (SEG_VARS, TOTAL_SEGS), jnp.float32, -0.2, 0.2) * steps_of(splits[9], (SEG_VARS, TOTAL_SEGS), ((1, 128),), -0.4, 0.0), -0.2, 0.2),
        "segment_to_perf": jnp.clip(jax.random.uniform(splits[10], (SEG_VARS, TOTAL_SEGS), jnp.float32, -0.15, 0.15) * steps_of(splits[10], (SEG_VARS, TOTAL_SEGS), ((1, 128),), -0.4, 0.0), -0.15, 0.15),
        "segment_source": scatter_about(splits[11], (SEG_VARS, TOTAL_SEGS), 1.0, 6.0, ((1, 128),), jnp.float32),
    }


def from_lower(values, direction):
    extent = values.shape[direction]
    zero_plane = jnp.zeros_like(lax.slice_in_dim(values, 0, 1, axis=direction))
    return jnp.concatenate([zero_plane, lax.slice_in_dim(values, 0, extent - 1, axis=direction)], axis=direction)


def from_upper(values, direction):
    extent = values.shape[direction]
    zero_plane = jnp.zeros_like(lax.slice_in_dim(values, 0, 1, axis=direction))
    return jnp.concatenate([lax.slice_in_dim(values, 1, extent, axis=direction), zero_plane], axis=direction)


def block_apply(blocks, vectors):
    return jnp.sum(blocks * vectors[None], axis=1)


def to_tiles(field):
    return field.reshape(N_GX, CX, N_GY, CY, NZ).transpose(0, 2, 1, 3, 4).reshape(DEVICES, CX * CY * NZ)


def from_tiles(blocks):
    return blocks.reshape(N_GX, N_GY, CX, CY, NZ).transpose(0, 2, 1, 3, 4).reshape(NX, NY, NZ)


def reference(source, cell_inverse, face_coefficients, tile_counts, perf_cells, segment_kinds, segment_inverse, upstream_coupling, downstream_coupling, perf_to_segment, segment_to_perf, segment_source):
    tile_rows = jnp.broadcast_to(jnp.arange(DEVICES, dtype=jnp.int32)[:, None, None], perf_cells.shape)
    used_slots = jnp.arange(CAP, dtype=jnp.int32)[None, None, :] < tile_counts[:, :, None]
    valid_mask = (segment_kinds != 0).astype(jnp.float32)
    linked = (segment_kinds == 2).astype(jnp.float32).reshape(DEVICES, SEG_DEV)
    unknowns = segment_source.shape[0]
    adjoint = jnp.zeros((NX, NY, NZ), jnp.float32)
    well_state = jnp.zeros(segment_source.shape, jnp.float32)
    for iteration in range(ITERS):
        inflow = from_lower(face_coefficients[0] * adjoint, 0) + from_upper(face_coefficients[1] * adjoint, 0)
        inflow = inflow + from_lower(face_coefficients[2] * adjoint, 1) + from_upper(face_coefficients[3] * adjoint, 1)
        inflow = inflow + from_lower(face_coefficients[4] * adjoint, 2) + from_upper(face_coefficients[5] * adjoint, 2)
        tile_field = to_tiles(adjoint)
        at_slots = jnp.where(used_slots, tile_field[tile_rows, perf_cells], 0.0)
        slot_values = at_slots.transpose(1, 0, 2).reshape(DEVICES * SEG_DEV)
        segment_terms = jnp.sum(segment_to_perf * well_state, axis=0)
        slot_terms = segment_terms.reshape(DEVICES, DEVICES, CAP).transpose(1, 0, 2)
        tile_terms = jnp.zeros((DEVICES, CX * CY * NZ), jnp.float32).at[tile_rows, perf_cells].add(slot_terms)
        well_cells = from_tiles(tile_terms)
        new_adjoint = cell_inverse * (source + inflow - well_cells)
        owned_state = well_state.reshape(unknowns, DEVICES, SEG_DEV)
        ahead_term = (jnp.roll(owned_state, -1, axis=2) * linked[None]).reshape(unknowns, DEVICES * SEG_DEV)
        behind_term = jnp.roll(owned_state * linked[None], 1, axis=2).reshape(unknowns, DEVICES * SEG_DEV)
        right_side = segment_source - perf_to_segment * slot_values[None] - block_apply(upstream_coupling, behind_term) - block_apply(downstream_coupling, ahead_term)
        well_state = valid_mask[None] * block_apply(segment_inverse, right_side)
        adjoint = new_adjoint
    return adjoint, well_state
```

```python
import functools

import jax
import jax.numpy as jnp
from jax import lax
from jax.experimental import pallas as pl
from jax.experimental.pallas import tpu as pltpu
from jax.sharding import PartitionSpec as P

ITERS = 8
F32 = jnp.float32
BF16 = jnp.bfloat16
AXES = ("gx", "gy")
CX, CY, NZ = 8, 64, 256
COLS = CX * CY
CAP, OWNERS = 32, 128
SLOTS = CAP * OWNERS
UP, DOWN, BASE, PERF, BACK, EDGE, BLOCKS = 0, 4, 8, 9, 10, 11, 12
VMEM = pl.BlockSpec(memory_space=pltpu.VMEM)


def run(kernel, operands, out_shape, flops=10**6, moved=10**6, scratch=()):
    many = isinstance(out_shape, (tuple, list))
    return pl.pallas_call(
        kernel,
        out_shape=out_shape,
        in_specs=[VMEM] * len(operands),
        out_specs=tuple(VMEM for _ in out_shape) if many else VMEM,
        scratch_shapes=list(scratch),
        compiler_params=pltpu.CompilerParams(vmem_limit_bytes=28 * 1024 * 1024),
        cost_estimate=pl.CostEstimate(flops=flops, bytes_accessed=moved, transcendentals=0),
    )(*operands)


def shape(*dims, dtype=F32):
    return jax.ShapeDtypeStruct(dims, dtype)


def iota(dims, axis):
    return lax.broadcasted_iota(jnp.int32, dims, axis)


def block_transpose(x):
    row = iota((128, 128), 0) & 3
    group = iota((128, 128), 1) >> 5
    y = x
    for d in range(1, 4):
        turned = jnp.where(row + d < 4, pltpu.roll(x, 128 - d, 0), pltpu.roll(x, 4 - d, 0))
        y = jnp.where(((group - row) & 3) == d, pltpu.roll(turned, 32 * d, 1), y)
    return y


def before(x):
    turned = pltpu.roll(x, 1, 1)
    return jnp.where(iota(x.shape, 1) == 0, pltpu.roll(turned, 1, 0), turned)


def after(x):
    turned = pltpu.roll(x, 127, 1)
    return jnp.where(iota(x.shape, 1) == 127, pltpu.roll(turned, x.shape[0] - 1, 0), turned)


def fold_kernel(kinds, inverse, upstream, downstream, perf, back, base, out, table):
    valid = (kinds[...] != 0).astype(F32)
    linked = (kinds[...] == 2).astype(F32)
    behind_mask = valid * before(linked)
    ahead_mask = valid * linked

    def plane(ref, a, b):
        return ref[pl.ds(a * 128 + b, 32, stride=4), :]

    def put(block, j, value):
        table[pl.ds(block * 128 + j, 32, stride=4), :] = value

    lane_slot = iota((32, 128), 1) & 31
    for a in range(4):
        row = [plane(inverse, a, c) for c in range(4)]

        def product(ref, b):
            return sum(row[c] * plane(ref, c, b) for c in range(4))

        for b in range(4):
            put(UP + a, b, behind_mask * product(upstream, b))
            put(DOWN + a, b, ahead_mask * product(downstream, b))
        start = valid * sum(row[c] * plane(base, 0, c) for c in range(4))
        put(BASE, a, start)
        put(PERF, a, valid * sum(row[c] * plane(perf, 0, c) for c in range(4)))
        put(BACK, a, plane(back, 0, a))
        put(EDGE, a, jnp.where(lane_slot == 0, before(start), after(start)))
    for block in range(BLOCKS):
        out[:, block * 128:(block + 1) * 128] = block_transpose(table[block * 128:(block + 1) * 128, :])


def hot_kernel(cells, hot):
    column = cells[...] >> 8
    index = iota((COLS, 128), 0)
    for k in range(CAP):
        hit = index == column[k:k + 1, :]
        hot[:, k * 128:(k + 1) * 128] = jnp.where(hit, 1.0, 0.0).astype(BF16)


def table_kernel(received, counts, table, state):
    used = ((iota((128, 128), 0) & 31) < counts[...]).astype(F32)
    for block in range(BLOCKS):
        part = received[:, block * 128:(block + 1) * 128].T
        if block == PERF:
            part = part * used
        if block == BASE:
            state[...] = part
        table[block * 128:(block + 1) * 128, :] = part


def parity_pair(parity, upper, lower):
    even = parity == 0
    return jnp.where(even, upper, lower), jnp.where(even, lower, upper)


def emit(cells, faces, state, x0, x1, r0, r1):
    gx, gy = lax.axis_index("gx"), lax.axis_index("gy")
    last, first = pl.ds(COLS - CY, CY), pl.ds(0, CY)
    x0[...], x1[...] = parity_pair(
        gx & 1, faces[0, last, :] * cells[last, :], faces[1, first, :] * cells[first, :])
    for x in range(CX):
        top, bottom = x * CY + CY - 1, x * CY
        r0[x:x + 1, :], r1[x:x + 1, :] = parity_pair(
            gy & 1, faces[2, top:top + 1, :] * cells[top:top + 1, :],
            faces[3, bottom:bottom + 1, :] * cells[bottom:bottom + 1, :])
    if state is not None:
        for v in range(4):
            r0[8 + v:9 + v, 0:128], r1[8 + v:9 + v, 0:128] = parity_pair(
                gy & 1, state[v * 32 + 31:v * 32 + 32, :], state[v * 32:v * 32 + 1, :])
    else:
        r0[8:16, :] = jnp.zeros((8, NZ), F32)
        r1[8:16, :] = jnp.zeros((8, NZ), F32)


def start_kernel(source, inverse, faces, cells, x0, x1, r0, r1):
    cells[...] = inverse[...] * source[...]
    emit(cells, faces, None, x0, x1, r0, r1)


def finish_kernel(first, last, inverse, faces, table, cells_in, state_in, x0, x1, r0, r1, cells, state, *out):
    gx, gy = lax.axis_index("gx"), lax.axis_index("gy")
    last_x, last_y = lax.axis_size("gx") - 1, lax.axis_size("gy") - 1
    cells[...] = cells_in[...]
    state[...] = state_in[...]
    upper, lower = parity_pair(gx & 1, x0[...], x1[...])
    top, bottom = pl.ds(COLS - CY, CY), pl.ds(0, CY)
    cells[top, :] = cells[top, :] + inverse[top, :] * jnp.where(gx < last_x, upper, 0.0)
    cells[bottom, :] = cells[bottom, :] + inverse[bottom, :] * jnp.where(gx > 0, lower, 0.0)
    upper, lower = parity_pair(gy & 1, r0[0:8, :], r1[0:8, :])
    upper, lower = jnp.where(gy < last_y, upper, 0.0), jnp.where(gy > 0, lower, 0.0)
    for x in range(CX):
        top, bottom = pl.ds(x * CY + CY - 1, 1), pl.ds(x * CY, 1)
        cells[top, :] = cells[top, :] + inverse[top, :] * upper[x:x + 1, :]
        cells[bottom, :] = cells[bottom, :] + inverse[bottom, :] * lower[x:x + 1, :]
    if first:
        high = [table[EDGE * 128 + v * 32 + 31:EDGE * 128 + v * 32 + 32, :] for v in range(4)]
        low = [table[EDGE * 128 + v * 32:EDGE * 128 + v * 32 + 1, :] for v in range(4)]
    else:
        pairs = [parity_pair(gy & 1, r0[8 + v:9 + v, 0:128], r1[8 + v:9 + v, 0:128]) for v in range(4)]
        high, low = [p[0] for p in pairs], [p[1] for p in pairs]
    for a in range(4):
        k = a * 32
        state[k:k + 1, :] = state[k:k + 1, :] - sum(
            table[(UP + a) * 128 + b * 32:(UP + a) * 128 + b * 32 + 1, :] * low[b] for b in range(4))
        k += 31
        state[k:k + 1, :] = state[k:k + 1, :] - sum(
            table[(DOWN + a) * 128 + b * 32 + 31:(DOWN + a) * 128 + b * 32 + 32, :] * high[b] for b in range(4))
    if last:
        out[0][...] = state[...].T
    else:
        emit(cells, faces, state, *out)


def sweep_kernel(slot_cells, hot, table, faces, inverse, source, cells, state, new_cells, new_state,
                 turned, spread, picked):
    height = slot_cells[...] & (NZ - 1)
    flipped = cells[...].T
    high = flipped.astype(BF16)
    turned[0:NZ, :] = high
    turned[NZ:2 * NZ, :] = (flipped - high.astype(F32)).astype(BF16)
    own = [state[v * 32:(v + 1) * 32, :] for v in range(4)]

    def coefficient(block, j):
        return table[block * 128 + j * 32:block * 128 + (j + 1) * 32, :]

    terms = sum(coefficient(BACK, v) * own[v] for v in range(4))
    level = iota((NZ, 128), 0)
    for k in range(CAP):
        part = pl.ds(k * 128, 128)
        hit = level == height[k:k + 1, :]
        term = terms[k:k + 1, :]
        term_high = term.astype(BF16).astype(F32)
        spread[0:NZ, part] = jnp.where(hit, term_high, 0.0).astype(BF16)
        spread[NZ:2 * NZ, part] = jnp.where(hit, term - term_high, 0.0).astype(BF16)
    for k in range(0, CAP, 2):
        both = jnp.dot(turned[...], hot[:, k * 128:(k + 2) * 128], preferred_element_type=F32)
        both = both[0:NZ] + both[NZ:2 * NZ]
        for h in range(2):
            hit = level == height[k + h:k + h + 1, :]
            picked[k + h:k + h + 1, :] = jnp.sum(
                jnp.where(hit, both[:, h * 128:(h + 1) * 128], 0.0), axis=0, keepdims=True)
    at_slots = picked[...]
    slot = iota((CAP, 128), 0)
    behind = [jnp.where(slot == 0, 0.0, pltpu.roll(v, 1, 0)) for v in own]
    ahead = [jnp.where(slot == CAP - 1, 0.0, pltpu.roll(v, CAP - 1, 0)) for v in own]
    for a in range(4):
        value = coefficient(BASE, a) - coefficient(PERF, a) * at_slots
        for b in range(4):
            value = value - coefficient(UP + a, b) * behind[b] - coefficient(DOWN + a, b) * ahead[b]
        new_state[a * 32:(a + 1) * 32, :] = value
    wells = lax.dot_general(hot[...], spread[...], (((1,), (1,)), ((), ())), preferred_element_type=F32)
    row, depth = iota((CY, NZ), 0), iota((CY, NZ), 1)
    for x in range(CX):
        here, down, up = (pl.ds(p * CY, CY) for p in (x, x - 1, x + 1))
        value = cells[here, :]
        total = source[here, :] - (wells[x * CY:(x + 1) * CY, 0:NZ] + wells[x * CY:(x + 1) * CY, NZ:2 * NZ])
        if x > 0:
            total = total + faces[0, down, :] * cells[down, :]
        if x < CX - 1:
            total = total + faces[1, up, :] * cells[up, :]
        total = total + jnp.where(row == 0, 0.0, pltpu.roll(faces[2, here, :] * value, 1, 0))
        total = total + jnp.where(row == CY - 1, 0.0, pltpu.roll(faces[3, here, :] * value, CY - 1, 0))
        total = total + jnp.where(depth == 0, 0.0, pltpu.roll(faces[4, here, :] * value, 1, 1))
        total = total + jnp.where(depth == NZ - 1, 0.0, pltpu.roll(faces[5, here, :] * value, NZ - 1, 1))
        new_cells[here, :] = inverse[here, :] * total


def unpack_kernel(received, out):
    out[...] = block_transpose(received[...])


def swap(value, axis, offset):
    count = lax.axis_size(axis)
    pairs = []
    for p in range(offset, count + offset, 2):
        a, b = p % count, (p + 1) % count
        pairs += [(a, b), (b, a)]
    return lax.ppermute(value, axis, pairs)


def exchange(x0, x1, r0, r1):
    return swap(x0, "gx", 0), swap(x1, "gx", 1), swap(r0, AXES, 0), swap(r1, AXES, 1)


def blocks_of(array):
    lead = array.shape[0] if array.ndim == 3 else 1
    return array.reshape(lead, 4, 32, 128).transpose(0, 2, 1, 3).reshape(lead * 128, 128)


def shards(source, cell_inverse, face_coefficients, tile_counts, perf_cells, segment_kinds, segment_inverse,
           upstream_coupling, downstream_coupling, perf_to_segment, segment_to_perf, segment_source):
    source = source.reshape(COLS, NZ)
    inverse = cell_inverse.reshape(COLS, NZ)
    faces = face_coefficients.reshape(6, COLS, NZ)
    slot_cells = perf_cells.reshape(OWNERS, CAP).T
    rims = (shape(CY, NZ), shape(CY, NZ), shape(16, NZ), shape(16, NZ))
    cells, *messages = run(start_kernel, (source, inverse, faces), (shape(COLS, NZ), *rims))
    messages = exchange(*messages)
    packed = run(
        fold_kernel,
        (segment_kinds.reshape(32, 128), blocks_of(segment_inverse), blocks_of(upstream_coupling),
         blocks_of(downstream_coupling), blocks_of(perf_to_segment), blocks_of(segment_to_perf),
         blocks_of(segment_source)),
        shape(128, BLOCKS * 128),
        scratch=[pltpu.VMEM((BLOCKS * 128, 128), F32)])
    received = lax.all_to_all(packed, AXES, split_axis=0, concat_axis=0, tiled=True)
    hot = run(hot_kernel, (slot_cells,), shape(COLS, SLOTS, dtype=BF16))
    table, state = run(
        table_kernel, (received, tile_counts), (shape(BLOCKS * 128, 128), shape(128, 128)))
    for sweep in range(1, ITERS):
        own_cells, own_state = run(
            sweep_kernel,
            (slot_cells, hot, table, faces, inverse, source, cells, state),
            (shape(COLS, NZ), shape(128, 128)),
            flops=4 * 10**9, moved=16 * 10**6,
            scratch=[pltpu.VMEM((2 * NZ, COLS), BF16), pltpu.VMEM((2 * NZ, SLOTS), BF16),
                     pltpu.VMEM((CAP, 128), F32)])
        last = sweep == ITERS - 1
        cells, state, *messages = run(
            functools.partial(finish_kernel, sweep == 1, last),
            (inverse, faces, table, own_cells, own_state, *messages),
            (shape(COLS, NZ), shape(128, 128), *((shape(128, 128),) if last else rims)))
        if not last:
            messages = exchange(*messages)
    returned = lax.all_to_all(messages[0], AXES, split_axis=0, concat_axis=0, tiled=True)
    states = run(unpack_kernel, (returned,), shape(128, 128))
    well_adjoint = states.reshape(32, 4, 128).transpose(1, 0, 2).reshape(4, 4096)
    return cells.reshape(CX, CY, NZ), well_adjoint


def solution(mesh):
    in_specs = (
        P("gx", "gy", None),
        P("gx", "gy", None),
        P(None, "gx", "gy", None),
        P(("gx", "gy"), None),
        P(("gx", "gy"), None, None),
        P(("gx", "gy")),
        P(None, None, ("gx", "gy")),
        P(None, None, ("gx", "gy")),
        P(None, None, ("gx", "gy")),
        P(None, ("gx", "gy")),
        P(None, ("gx", "gy")),
        P(None, ("gx", "gy")),
    )
    out_specs = (P("gx", "gy", None), P(None, ("gx", "gy")))
    return jax.shard_map(shards, mesh=mesh, in_specs=in_specs, out_specs=out_specs, check_vma=False)
```

```python
import functools

import jax
import jax.numpy as jnp
from jax import lax
from jax.experimental import pallas as pl
from jax.experimental.pallas import tpu as pltpu
from jax.sharding import PartitionSpec as P

ITERS = 8
F32 = jnp.float32
BF16 = jnp.bfloat16
AXES = ("gx", "gy")
CX, CY, NZ = 8, 64, 256
COLS = CX * CY
CAP, OWNERS = 32, 128
SLOTS = CAP * OWNERS
UP, DOWN, BASE, PERF, BACK, EDGE, BLOCKS = 0, 4, 8, 9, 10, 11, 12
VMEM = pl.BlockSpec(memory_space=pltpu.VMEM)
FAR = pl.BlockSpec(memory_space=pl.ANY)


def run(kernel, operands, out_shape, flops=10**6, moved=10**6, scratch=(), far=0, far_out=0, limit=28):
    many = isinstance(out_shape, (tuple, list))
    operands = [pltpu.with_memory_space_constraint(o, pltpu.HBM) if i < far else o for i, o in enumerate(operands)]
    return pl.pallas_call(
        kernel,
        out_shape=out_shape,
        in_specs=[FAR] * far + [VMEM] * (len(operands) - far),
        out_specs=tuple(FAR if i < far_out else VMEM for i in range(len(out_shape))) if many else VMEM,
        scratch_shapes=list(scratch),
        compiler_params=pltpu.CompilerParams(vmem_limit_bytes=limit * 1024 * 1024),
        cost_estimate=pl.CostEstimate(flops=flops, bytes_accessed=moved, transcendentals=0),
    )(*operands)


def bring(sources, targets, semaphores):
    copies = [pltpu.make_async_copy(a, b, semaphores.at[i]) for i, (a, b) in enumerate(zip(sources, targets))]
    for copy in copies:
        copy.start()
    return copies


def shape(*dims, dtype=F32):
    return jax.ShapeDtypeStruct(dims, dtype)


def iota(dims, axis):
    return lax.broadcasted_iota(jnp.int32, dims, axis)


def block_transpose(x):
    row = iota((128, 128), 0) & 3
    group = iota((128, 128), 1) >> 5
    y = x
    for d in range(1, 4):
        turned = jnp.where(row + d < 4, pltpu.roll(x, 128 - d, 0), pltpu.roll(x, 4 - d, 0))
        y = jnp.where(((group - row) & 3) == d, pltpu.roll(turned, 32 * d, 1), y)
    return y


def before(x):
    turned = pltpu.roll(x, 1, 1)
    return jnp.where(iota(x.shape, 1) == 0, pltpu.roll(turned, 1, 0), turned)


def after(x):
    turned = pltpu.roll(x, 127, 1)
    return jnp.where(iota(x.shape, 1) == 127, pltpu.roll(turned, x.shape[0] - 1, 0), turned)


def fold_kernel(*refs):
    far, out, table, near, semaphores = refs[:7], refs[7], refs[8], refs[9:16], refs[16]
    for copy in bring(far, near, semaphores):
        copy.wait()
    kinds, inverse, upstream, downstream, perf, back, base = near
    valid = (kinds[...] != 0).astype(F32)
    linked = (kinds[...] == 2).astype(F32)
    behind_mask = valid * before(linked)
    ahead_mask = valid * linked

    def plane(ref, a, b):
        return ref[pl.ds(a * 128 + b, 32, stride=4), :]

    def put(block, j, value):
        table[pl.ds(block * 128 + j, 32, stride=4), :] = value

    lane_slot = iota((32, 128), 1) & 31
    for a in range(4):
        row = [plane(inverse, a, c) for c in range(4)]

        def product(ref, b):
            return sum(row[c] * plane(ref, c, b) for c in range(4))

        for b in range(4):
            put(UP + a, b, behind_mask * product(upstream, b))
            put(DOWN + a, b, ahead_mask * product(downstream, b))
        start = valid * sum(row[c] * plane(base, 0, c) for c in range(4))
        put(BASE, a, start)
        put(PERF, a, valid * sum(row[c] * plane(perf, 0, c) for c in range(4)))
        put(BACK, a, plane(back, 0, a))
        put(EDGE, a, jnp.where(lane_slot == 0, before(start), after(start)))
    for block in range(BLOCKS):
        out[pl.ds(block, 128, stride=BLOCKS), :] = block_transpose(table[block * 128:(block + 1) * 128, :])


def make_hot(slot_cells, hot):
    column = slot_cells[...] >> 8
    index = iota((COLS, 128), 0)
    for k in range(CAP):
        hit = index == column[k:k + 1, :]
        hot[:, k * 128:(k + 1) * 128] = jnp.where(hit, 1.0, 0.0).astype(BF16)


def make_table(received, counts, table, state):
    used = ((iota((128, 128), 0) & 31) < counts[...]).astype(F32)
    for block in range(BLOCKS):
        part = received[pl.ds(block, 128, stride=BLOCKS), :].T
        if block == PERF:
            part = part * used
        if block == BASE:
            state[...] = part
        table[block * 128:(block + 1) * 128, :] = part


def parity_pair(parity, upper, lower):
    even = parity == 0
    return jnp.where(even, upper, lower), jnp.where(even, lower, upper)


def emit(cells, faces, state, x0, x1, r0, r1):
    gx, gy = lax.axis_index("gx"), lax.axis_index("gy")
    last, first = pl.ds(COLS - CY, CY), pl.ds(0, CY)
    x0[...], x1[...] = parity_pair(
        gx & 1, faces[0, last, :] * cells[last, :], faces[1, first, :] * cells[first, :])
    for x in range(CX):
        top, bottom = x * CY + CY - 1, x * CY
        r0[x:x + 1, :], r1[x:x + 1, :] = parity_pair(
            gy & 1, faces[2, top:top + 1, :] * cells[top:top + 1, :],
            faces[3, bottom:bottom + 1, :] * cells[bottom:bottom + 1, :])
    if state is not None:
        for v in range(4):
            r0[8 + v:9 + v, 0:128], r1[8 + v:9 + v, 0:128] = parity_pair(
                gy & 1, state[v * 32 + 31:v * 32 + 32, :], state[v * 32:v * 32 + 1, :])
    else:
        r0[8:16, :] = jnp.zeros((8, NZ), F32)
        r1[8:16, :] = jnp.zeros((8, NZ), F32)


def start_kernel(far_source, far_inverse, far_faces, x0, x1, r0, r1, source, inverse, faces, cells, semaphores):
    copies = bring((far_source, far_inverse, far_faces), (source, inverse, faces), semaphores)
    for copy in copies[:2]:
        copy.wait()
    cells[...] = inverse[...] * source[...]
    copies[2].wait()
    emit(cells, faces, None, x0, x1, r0, r1)


def finish_cells(inverse, cells_in, x0, x1, r0, r1, cells):
    gx, gy = lax.axis_index("gx"), lax.axis_index("gy")
    last_x, last_y = lax.axis_size("gx") - 1, lax.axis_size("gy") - 1
    cells[...] = cells_in[...]
    upper, lower = parity_pair(gx & 1, x0[...], x1[...])
    top, bottom = pl.ds(COLS - CY, CY), pl.ds(0, CY)
    cells[top, :] = cells[top, :] + inverse[top, :] * jnp.where(gx < last_x, upper, 0.0)
    cells[bottom, :] = cells[bottom, :] + inverse[bottom, :] * jnp.where(gx > 0, lower, 0.0)
    upper, lower = parity_pair(gy & 1, r0[0:8, :], r1[0:8, :])
    upper, lower = jnp.where(gy < last_y, upper, 0.0), jnp.where(gy > 0, lower, 0.0)
    for x in range(CX):
        top, bottom = pl.ds(x * CY + CY - 1, 1), pl.ds(x * CY, 1)
        cells[top, :] = cells[top, :] + inverse[top, :] * upper[x:x + 1, :]
        cells[bottom, :] = cells[bottom, :] + inverse[bottom, :] * lower[x:x + 1, :]


def finish_state(first, table, state_in, r0, r1, state):
    gy = lax.axis_index("gy")
    state[...] = state_in[...]
    if first:
        high = [table[EDGE * 128 + v * 32 + 31:EDGE * 128 + v * 32 + 32, :] for v in range(4)]
        low = [table[EDGE * 128 + v * 32:EDGE * 128 + v * 32 + 1, :] for v in range(4)]
    else:
        pairs = [parity_pair(gy & 1, r0[8 + v:9 + v, 0:128], r1[8 + v:9 + v, 0:128]) for v in range(4)]
        high, low = [p[0] for p in pairs], [p[1] for p in pairs]
    for a in range(4):
        k = a * 32
        state[k:k + 1, :] = state[k:k + 1, :] - sum(
            table[(UP + a) * 128 + b * 32:(UP + a) * 128 + b * 32 + 1, :] * low[b] for b in range(4))
        k += 31
        state[k:k + 1, :] = state[k:k + 1, :] - sum(
            table[(DOWN + a) * 128 + b * 32 + 31:(DOWN + a) * 128 + b * 32 + 32, :] * high[b] for b in range(4))


def finish_kernel(first, inverse, faces, table, cells_in, state_in, x0, x1, r0, r1, cells, state, *out):
    finish_state(first, table, state_in, r0, r1, state)
    finish_cells(inverse, cells_in, x0, x1, r0, r1, cells)
    emit(cells, faces, state, *out)


def finish_state_kernel(table, state_in, r0, r1, out, state):
    finish_state(False, table, state_in, r0, r1, state)
    out[...] = state[...].T


def pick(slot_cells, hot, cells, turned, picked):
    height = slot_cells[...] & (NZ - 1)
    flipped = cells[...].T
    high = flipped.astype(BF16)
    turned[0:NZ, :] = high
    turned[NZ:2 * NZ, :] = (flipped - high.astype(F32)).astype(BF16)
    level = iota((NZ, 128), 0)
    for k in range(0, CAP, 2):
        both = jnp.dot(turned[...], hot[:, k * 128:(k + 2) * 128], preferred_element_type=F32)
        both = both[0:NZ] + both[NZ:2 * NZ]
        for h in range(2):
            hit = level == height[k + h:k + h + 1, :]
            picked[k + h:k + h + 1, :] = jnp.sum(
                jnp.where(hit, both[:, h * 128:(h + 1) * 128], 0.0), axis=0, keepdims=True)


def coefficient(table, block, j):
    return table[block * 128 + j * 32:block * 128 + (j + 1) * 32, :]


def advance(table, state, at_slots, new_state):
    own = [state[v * 32:(v + 1) * 32, :] for v in range(4)]
    slot = iota((CAP, 128), 0)
    behind = [jnp.where(slot == 0, 0.0, pltpu.roll(v, 1, 0)) for v in own]
    ahead = [jnp.where(slot == CAP - 1, 0.0, pltpu.roll(v, CAP - 1, 0)) for v in own]
    for a in range(4):
        value = coefficient(table, BASE, a) - coefficient(table, PERF, a) * at_slots
        for b in range(4):
            value = value - coefficient(table, UP + a, b) * behind[b] - coefficient(table, DOWN + a, b) * ahead[b]
        new_state[a * 32:(a + 1) * 32, :] = value


def make_spread(slot_cells, table, state, spread):
    height = slot_cells[...] & (NZ - 1)
    terms = sum(coefficient(table, BACK, v) * state[v * 32:(v + 1) * 32, :] for v in range(4))
    level = iota((NZ, 128), 0)
    for k in range(CAP):
        part = pl.ds(k * 128, 128)
        hit = level == height[k:k + 1, :]
        term = terms[k:k + 1, :]
        term_high = term.astype(BF16).astype(F32)
        spread[0:NZ, part] = jnp.where(hit, term_high, 0.0).astype(BF16)
        spread[NZ:2 * NZ, part] = jnp.where(hit, term - term_high, 0.0).astype(BF16)


def gather_spread(hot, spread):
    return lax.dot_general(hot[...], spread[...], (((1,), (1,)), ((), ())), preferred_element_type=F32)


def scatter(slot_cells, hot, table, state, spread):
    make_spread(slot_cells, table, state, spread)
    return gather_spread(hot, spread)


def inflow(faces, source, cells, x):
    row, depth = iota((CY, NZ), 0), iota((CY, NZ), 1)
    here, down, up = (pl.ds(p * CY, CY) for p in (x, x - 1, x + 1))
    value = cells[here, :]
    total = source[here, :]
    if x > 0:
        total = total + faces[0, down, :] * cells[down, :]
    if x < CX - 1:
        total = total + faces[1, up, :] * cells[up, :]
    total = total + jnp.where(row == 0, 0.0, pltpu.roll(faces[2, here, :] * value, 1, 0))
    total = total + jnp.where(row == CY - 1, 0.0, pltpu.roll(faces[3, here, :] * value, CY - 1, 0))
    total = total + jnp.where(depth == 0, 0.0, pltpu.roll(faces[4, here, :] * value, 1, 1))
    return total + jnp.where(depth == NZ - 1, 0.0, pltpu.roll(faces[5, here, :] * value, NZ - 1, 1))


def well_plane(wells, x):
    return wells[x * CY:(x + 1) * CY, 0:NZ] + wells[x * CY:(x + 1) * CY, NZ:2 * NZ]


def sweep_kernel(slot_cells, hot, table, faces, inverse, source, cells, state, new_cells, new_state,
                 turned, spread, picked):
    pick(slot_cells, hot, cells, turned, picked)
    advance(table, state, picked[...], new_state)
    wells = scatter(slot_cells, hot, table, state, spread)
    for x in range(CX):
        here = pl.ds(x * CY, CY)
        new_cells[here, :] = inverse[here, :] * (inflow(faces, source, cells, x) - well_plane(wells, x))


def first_kernel(far_source, far_inverse, slot_cells, far_hot, picked, source, inverse, hot, turned, semaphores):
    copies = bring((far_source, far_inverse), (source, inverse), semaphores)
    make_hot(slot_cells, hot)
    store = pltpu.make_async_copy(hot, far_hot, semaphores.at[2])
    store.start()
    for copy in copies:
        copy.wait()
    source[...] = inverse[...] * source[...]
    pick(slot_cells, hot, source, turned, picked)
    store.wait()


def second_kernel(far_received, far_hot, far_source, far_inverse, far_faces, slot_cells, counts, picked,
                  table, hot, source, inverse, faces, new_cells, new_state, received, spread, cells, state, semaphores):
    copies = bring(
        (far_received, far_hot, far_source, far_inverse, far_faces), (received, hot, source, inverse, faces), semaphores)
    copies[0].wait()
    make_table(received, counts, table, state)
    advance(table, state, picked[...], new_state)
    make_spread(slot_cells, table, state, spread)
    copies[1].wait()
    wells = gather_spread(hot, spread)
    for copy in copies[2:]:
        copy.wait()
    cells[...] = inverse[...] * source[...]
    for x in range(CX):
        here = pl.ds(x * CY, CY)
        new_cells[here, :] = inverse[here, :] * (inflow(faces, source, cells, x) - well_plane(wells, x))


def last_state_kernel(slot_cells, hot, table, cells, state, new_state, turned, picked):
    pick(slot_cells, hot, cells, turned, picked)
    advance(table, state, picked[...], new_state)


def last_cells_kernel(slot_cells, hot, table, faces, inverse, source, cells, state, x0, x1, r0, r1, new_cells,
                      spread, own_cells):
    wells = scatter(slot_cells, hot, table, state, spread)
    for x in range(CX):
        here = pl.ds(x * CY, CY)
        own_cells[here, :] = inverse[here, :] * (inflow(faces, source, cells, x) - well_plane(wells, x))
    finish_cells(inverse, own_cells, x0, x1, r0, r1, new_cells)


def unpack_kernel(received, out):
    out[...] = block_transpose(received[...])


def swap(value, axis, offset):
    count = lax.axis_size(axis)
    pairs = []
    for p in range(offset, count + offset, 2):
        a, b = p % count, (p + 1) % count
        pairs += [(a, b), (b, a)]
    return lax.ppermute(value, axis, pairs)


def all_to_all(rows):
    sent = rows.reshape(128, -1)
    return lax.all_to_all(sent, AXES, split_axis=0, concat_axis=0, tiled=True).reshape(rows.shape)


def exchange(x0, x1, r0, r1):
    return swap(x0, "gx", 0), swap(x1, "gx", 1), swap(r0, AXES, 0), swap(r1, AXES, 1)


def blocks_of(array):
    lead = array.shape[0] if array.ndim == 3 else 1
    return array.reshape(lead, 4, 32, 128).transpose(0, 2, 1, 3).reshape(lead * 128, 128)


def shards(source, cell_inverse, face_coefficients, tile_counts, perf_cells, segment_kinds, segment_inverse,
           upstream_coupling, downstream_coupling, perf_to_segment, segment_to_perf, segment_source):
    source = source.reshape(COLS, NZ)
    inverse = cell_inverse.reshape(COLS, NZ)
    faces = face_coefficients.reshape(6, COLS, NZ)
    slot_cells = perf_cells.reshape(OWNERS, CAP).T
    field, planes = shape(COLS, NZ), shape(128, 128)
    rims = (shape(CY, NZ), shape(CY, NZ), shape(16, NZ), shape(16, NZ))
    turned, spread = pltpu.VMEM((2 * NZ, COLS), BF16), pltpu.VMEM((2 * NZ, SLOTS), BF16)
    picked = pltpu.VMEM((CAP, 128), F32)
    half = dict(flops=2 * 10**9, moved=8 * 10**6)
    whole = dict(flops=4 * 10**9, moved=16 * 10**6)

    operands = (segment_kinds.reshape(32, 128), blocks_of(segment_inverse), blocks_of(upstream_coupling),
                blocks_of(downstream_coupling), blocks_of(perf_to_segment), blocks_of(segment_to_perf),
                blocks_of(segment_source))
    packed = run(
        fold_kernel, operands, shape(BLOCKS * 128, 128), far=7, limit=56,
        scratch=[pltpu.VMEM((BLOCKS * 128, 128), F32), *(pltpu.VMEM(o.shape, o.dtype) for o in operands),
                 pltpu.SemaphoreType.DMA((7,))])
    received = all_to_all(packed)
    near_field, near_faces = pltpu.VMEM((COLS, NZ), F32), pltpu.VMEM((6, COLS, NZ), F32)
    messages = run(
        start_kernel, (source, inverse, faces), rims, far=3, limit=56,
        scratch=[near_field, near_field, near_faces, near_field, pltpu.SemaphoreType.DMA((3,))])
    messages = exchange(*messages)
    hot_shape = shape(COLS, SLOTS, dtype=BF16)
    far_hot, at_slots = run(
        first_kernel, (source, inverse, slot_cells), (hot_shape, shape(CAP, 128)), far=2, far_out=1, limit=56,
        scratch=[near_field, near_field, pltpu.VMEM(hot_shape.shape, BF16), turned, pltpu.SemaphoreType.DMA((3,))],
        **half)
    table, hot, source, inverse, faces, own_cells, own_state = run(
        second_kernel, (received, far_hot, source, inverse, faces, slot_cells, tile_counts, at_slots),
        (shape(BLOCKS * 128, 128), hot_shape, field, field, shape(6, COLS, NZ), field, planes), far=5,
        scratch=[pltpu.VMEM((BLOCKS * 128, 128), F32), spread, near_field, pltpu.VMEM((128, 128), F32),
                 pltpu.SemaphoreType.DMA((5,))], **half)
    for sweep in range(1, ITERS - 1):
        cells, state, *messages = run(
            functools.partial(finish_kernel, sweep == 1),
            (inverse, faces, table, own_cells, own_state, *messages), (field, planes, *rims))
        messages = exchange(*messages)
        if sweep < ITERS - 2:
            own_cells, own_state = run(
                sweep_kernel, (slot_cells, hot, table, faces, inverse, source, cells, state), (field, planes),
                scratch=[turned, spread, picked], **whole)
    own_state = run(
        last_state_kernel, (slot_cells, hot, table, cells, state), planes, scratch=[turned, picked], **half)
    packed = run(
        finish_state_kernel, (table, own_state, *messages[2:]), planes, scratch=[pltpu.VMEM((128, 128), F32)])
    returned = all_to_all(packed)
    cells = run(
        last_cells_kernel, (slot_cells, hot, table, faces, inverse, source, cells, state, *messages), field,
        scratch=[spread, pltpu.VMEM((COLS, NZ), F32)], **half)
    states = run(unpack_kernel, (returned,), planes)
    well_adjoint = states.reshape(32, 4, 128).transpose(1, 0, 2).reshape(4, 4096)
    return cells.reshape(CX, CY, NZ), well_adjoint


def solution(mesh):
    in_specs = (
        P("gx", "gy", None),
        P("gx", "gy", None),
        P(None, "gx", "gy", None),
        P(("gx", "gy"), None),
        P(("gx", "gy"), None, None),
        P(("gx", "gy")),
        P(None, None, ("gx", "gy")),
        P(None, None, ("gx", "gy")),
        P(None, None, ("gx", "gy")),
        P(None, ("gx", "gy")),
        P(None, ("gx", "gy")),
        P(None, ("gx", "gy")),
    )
    out_specs = (P("gx", "gy", None), P(None, ("gx", "gy")))
    return jax.shard_map(shards, mesh=mesh, in_specs=in_specs, out_specs=out_specs, check_vma=False)
```

```python
import functools

import jax
import jax.numpy as jnp
from jax import lax
from jax.experimental import pallas as pl
from jax.experimental.pallas import tpu as pltpu
from jax.sharding import PartitionSpec as P

ITERS = 8
F32 = jnp.float32
BF16 = jnp.bfloat16
AXES = ("gx", "gy")
CX, CY, NZ = 8, 64, 256
COLS = CX * CY
CAP, OWNERS = 32, 128
SLOTS = CAP * OWNERS
BLOCK = 8 * CAP
GROUPS = SLOTS // BLOCK
FEW = 10
UP, DOWN, BASE, PERF, BACK, EDGE, BLOCKS = 0, 4, 8, 9, 10, 11, 12
VMEM = pl.BlockSpec(memory_space=pltpu.VMEM)
FAR = pl.BlockSpec(memory_space=pl.ANY)


def run(kernel, operands, out_shape, flops=10**6, moved=10**6, scratch=(), far=0, far_out=0, limit=28):
    many = isinstance(out_shape, (tuple, list))
    operands = [pltpu.with_memory_space_constraint(o, pltpu.HBM) if i < far else o for i, o in enumerate(operands)]
    return pl.pallas_call(
        kernel,
        out_shape=out_shape,
        in_specs=[FAR] * far + [VMEM] * (len(operands) - far),
        out_specs=tuple(FAR if i < far_out else VMEM for i in range(len(out_shape))) if many else VMEM,
        scratch_shapes=list(scratch),
        compiler_params=pltpu.CompilerParams(vmem_limit_bytes=limit * 1024 * 1024),
        cost_estimate=pl.CostEstimate(flops=flops, bytes_accessed=moved, transcendentals=0),
    )(*operands)


def bring(sources, targets, semaphores):
    copies = [pltpu.make_async_copy(a, b, semaphores.at[i]) for i, (a, b) in enumerate(zip(sources, targets))]
    for copy in copies:
        copy.start()
    return copies


def shape(*dims, dtype=F32):
    return jax.ShapeDtypeStruct(dims, dtype)


def iota(dims, axis):
    return lax.broadcasted_iota(jnp.int32, dims, axis)


def block_transpose(x):
    row = iota((128, 128), 0) & 3
    group = iota((128, 128), 1) >> 5
    y = x
    for d in range(1, 4):
        turned = jnp.where(row + d < 4, pltpu.roll(x, 128 - d, 0), pltpu.roll(x, 4 - d, 0))
        y = jnp.where(((group - row) & 3) == d, pltpu.roll(turned, 32 * d, 1), y)
    return y


def before(x):
    turned = pltpu.roll(x, 1, 1)
    return jnp.where(iota(x.shape, 1) == 0, pltpu.roll(turned, 1, 0), turned)


def after(x):
    turned = pltpu.roll(x, 127, 1)
    return jnp.where(iota(x.shape, 1) == 127, pltpu.roll(turned, x.shape[0] - 1, 0), turned)


def fold_kernel(*refs):
    far, out, table, near, semaphores = refs[:7], refs[7], refs[8], refs[9:16], refs[16]
    for copy in bring(far, near, semaphores):
        copy.wait()
    kinds, inverse, upstream, downstream, perf, back, base = near
    valid = (kinds[...] != 0).astype(F32)
    linked = (kinds[...] == 2).astype(F32)
    behind_mask = valid * before(linked)
    ahead_mask = valid * linked

    def plane(ref, a, b):
        return ref[pl.ds(a * 128 + b, 32, stride=4), :]

    def put(block, j, value):
        table[pl.ds(block * 128 + j, 32, stride=4), :] = value

    lane_slot = iota((32, 128), 1) & 31
    for a in range(4):
        row = [plane(inverse, a, c) for c in range(4)]

        def product(ref, b):
            return sum(row[c] * plane(ref, c, b) for c in range(4))

        for b in range(4):
            put(UP + a, b, behind_mask * product(upstream, b))
            put(DOWN + a, b, ahead_mask * product(downstream, b))
        start = valid * sum(row[c] * plane(base, 0, c) for c in range(4))
        put(BASE, a, start)
        put(PERF, a, valid * sum(row[c] * plane(perf, 0, c) for c in range(4)))
        put(BACK, a, plane(back, 0, a))
        put(EDGE, a, jnp.where(lane_slot == 0, before(start), after(start)))
    for block in range(BLOCKS):
        out[pl.ds(block, 128, stride=BLOCKS), :] = block_transpose(table[block * 128:(block + 1) * 128, :])


def owner_order(counts):
    active = (counts[...] > 0).astype(F32)
    earlier = (iota((OWNERS, OWNERS), 0) < iota((OWNERS, OWNERS), 1)).astype(BF16)
    place = jnp.dot(active.astype(BF16), earlier, preferred_element_type=F32).astype(jnp.int32)
    order = jnp.where((iota((OWNERS, OWNERS), 0) == place) & (active > 0.0), 1.0, 0.0)
    return order.astype(BF16)


def pack(high, low, order, page):
    both = jnp.concatenate([high, low], axis=0).astype(BF16)
    packed = lax.dot_general(both, order, (((1,), (1,)), ((), ())), preferred_element_type=F32)
    page[:, 0:2 * CAP] = packed.T
    group = iota((GROUPS, 128), 1) >> 5
    results = []
    for part in range(2):
        halves = []
        for half in range(2):
            total = None
            for g in range(4):
                rows = page[pl.ds(half * 4 + g, GROUPS, stride=8), :]
                shift = (32 * (g - part)) % 128
                rows = pltpu.roll(rows, shift, 1) if shift else rows
                total = rows if total is None else jnp.where(group == g, rows, total)
            halves.append(total)
        results.append(jnp.concatenate(halves, axis=1))
    return results


def unpack(rows, order, page):
    for q in range(8):
        part = rows[:, (q // 4) * 128:(q // 4 + 1) * 128]
        shift = (128 - 32 * (q % 4)) % 128
        page[pl.ds(q, GROUPS, stride=8), :] = pltpu.roll(part, shift, 1) if shift else part
    plane = page[...].T[0:CAP, :]
    high = plane.astype(BF16)
    both = jnp.concatenate([high, (plane - high.astype(F32)).astype(BF16)], axis=0)
    placed = jnp.dot(both, order[...], preferred_element_type=F32)
    return placed[0:CAP] + placed[CAP:2 * CAP]


def pack_slots(slot_cells, order, columns, heights, page):
    column = slot_cells[...] >> 8
    high, low = pack((column & 510).astype(F32), (column & 1).astype(F32), order[...], page)
    columns[...] = (high + low).astype(jnp.int32)
    height = (slot_cells[...] & (NZ - 1)).astype(F32)
    heights[...] = pack(height, jnp.zeros_like(height), order[...], page)[0].astype(jnp.int32)


def make_hot(blocks, columns, hot):
    index = iota((COLS, BLOCK), 0)
    for b in blocks:
        hit = index == columns[b:b + 1, :]
        hot[:, b * BLOCK:(b + 1) * BLOCK] = jnp.where(hit, 1.0, 0.0).astype(BF16)


def make_rest(columns, hot):
    @pl.loop(FEW, GROUPS)
    def _(b):
        hit = iota((COLS, BLOCK), 0) == columns[pl.ds(b, 1), :]
        hot[:, pl.ds(pl.multiple_of(b * BLOCK, BLOCK), BLOCK)] = jnp.where(hit, 1.0, 0.0).astype(BF16)


def by_number(counts, few, many):
    active = jnp.sum((counts[...] > 0).astype(jnp.int32))
    pl.when(active > 8 * FEW)(many)
    pl.when(active <= 8 * FEW)(few)


def make_table(blocks, received, counts, table, state):
    used = ((iota((128, 128), 0) & 31) < counts[...]).astype(F32)
    for block in blocks:
        part = received[pl.ds(block, 128, stride=BLOCKS), :].T
        if block == PERF:
            part = part * used
        if block == BASE:
            state[...] = part
        table[block * 128:(block + 1) * 128, :] = part


def parity_pair(parity, upper, lower):
    even = parity == 0
    return jnp.where(even, upper, lower), jnp.where(even, lower, upper)


def emit(cells, faces, state, x0, x1, r0, r1):
    gx, gy = lax.axis_index("gx"), lax.axis_index("gy")
    last, first = pl.ds(COLS - CY, CY), pl.ds(0, CY)
    x0[...], x1[...] = parity_pair(
        gx & 1, faces[0, last, :] * cells[last, :], faces[1, first, :] * cells[first, :])
    for x in range(CX):
        top, bottom = x * CY + CY - 1, x * CY
        r0[x:x + 1, :], r1[x:x + 1, :] = parity_pair(
            gy & 1, faces[2, top:top + 1, :] * cells[top:top + 1, :],
            faces[3, bottom:bottom + 1, :] * cells[bottom:bottom + 1, :])
    if state is not None:
        for v in range(4):
            r0[8 + v:9 + v, 0:128], r1[8 + v:9 + v, 0:128] = parity_pair(
                gy & 1, state[v * 32 + 31:v * 32 + 32, :], state[v * 32:v * 32 + 1, :])
    else:
        r0[8:16, :] = jnp.zeros((8, NZ), F32)
        r1[8:16, :] = jnp.zeros((8, NZ), F32)


def start_kernel(far_source, far_inverse, far_faces, x0, x1, r0, r1, source, inverse, faces, cells, semaphores):
    top, bottom = pl.ds(COLS - CY, CY), pl.ds(0, CY)
    parts = [(0, top), (1, bottom), (2, pl.ds(0, COLS)), (3, pl.ds(0, COLS))]
    copies = bring(
        [far_source, far_inverse] + [far_faces.at[f, rows, :] for f, rows in parts],
        [source, inverse] + [faces.at[f, rows, :] for f, rows in parts], semaphores)
    for copy in copies[:2]:
        copy.wait()
    cells[...] = inverse[...] * source[...]
    for copy in copies[2:]:
        copy.wait()
    emit(cells, faces, None, x0, x1, r0, r1)


def finish_cells(inverse, cells_in, x0, x1, r0, r1, cells):
    gx, gy = lax.axis_index("gx"), lax.axis_index("gy")
    last_x, last_y = lax.axis_size("gx") - 1, lax.axis_size("gy") - 1
    cells[...] = cells_in[...]
    upper, lower = parity_pair(gx & 1, x0[...], x1[...])
    top, bottom = pl.ds(COLS - CY, CY), pl.ds(0, CY)
    cells[top, :] = cells[top, :] + inverse[top, :] * jnp.where(gx < last_x, upper, 0.0)
    cells[bottom, :] = cells[bottom, :] + inverse[bottom, :] * jnp.where(gx > 0, lower, 0.0)
    upper, lower = parity_pair(gy & 1, r0[0:8, :], r1[0:8, :])
    upper, lower = jnp.where(gy < last_y, upper, 0.0), jnp.where(gy > 0, lower, 0.0)
    for x in range(CX):
        top, bottom = pl.ds(x * CY + CY - 1, 1), pl.ds(x * CY, 1)
        cells[top, :] = cells[top, :] + inverse[top, :] * upper[x:x + 1, :]
        cells[bottom, :] = cells[bottom, :] + inverse[bottom, :] * lower[x:x + 1, :]


def finish_state(first, table, state_in, r0, r1, state):
    gy = lax.axis_index("gy")
    state[...] = state_in[...]
    if first:
        high = [table[EDGE * 128 + v * 32 + 31:EDGE * 128 + v * 32 + 32, :] for v in range(4)]
        low = [table[EDGE * 128 + v * 32:EDGE * 128 + v * 32 + 1, :] for v in range(4)]
    else:
        pairs = [parity_pair(gy & 1, r0[8 + v:9 + v, 0:128], r1[8 + v:9 + v, 0:128]) for v in range(4)]
        high, low = [p[0] for p in pairs], [p[1] for p in pairs]
    for a in range(4):
        k = a * 32
        state[k:k + 1, :] = state[k:k + 1, :] - sum(
            table[(UP + a) * 128 + b * 32:(UP + a) * 128 + b * 32 + 1, :] * low[b] for b in range(4))
        k += 31
        state[k:k + 1, :] = state[k:k + 1, :] - sum(
            table[(DOWN + a) * 128 + b * 32 + 31:(DOWN + a) * 128 + b * 32 + 32, :] * high[b] for b in range(4))


def finish_kernel(first, inverse, faces, table, cells_in, state_in, x0, x1, r0, r1, cells, state, *out):
    finish_state(first, table, state_in, r0, r1, state)
    finish_cells(inverse, cells_in, x0, x1, r0, r1, cells)
    emit(cells, faces, state, *out)


def last_kernel(table, state_in, r0, r1, inverse, cells_in, x0, x1, cells, out, state):
    finish_cells(inverse, cells_in, x0, x1, r0, r1, cells)
    finish_state(False, table, state_in, r0, r1, state)
    out[...] = state[...].T


def turn(cells, turned):
    flipped = cells[...].T
    high = flipped.astype(BF16)
    turned[0:NZ, :] = high
    turned[NZ:2 * NZ, :] = (flipped - high.astype(F32)).astype(BF16)


def pick_block(b, heights, hot, turned, picked):
    here = pl.ds(b * BLOCK, BLOCK) if isinstance(b, int) else pl.ds(pl.multiple_of(b * BLOCK, BLOCK), BLOCK)
    both = jnp.dot(turned[...], hot[:, here], preferred_element_type=F32)
    hit = iota((NZ, BLOCK), 0) == heights[pl.ds(b, 1), :]
    picked[pl.ds(b, 1), :] = jnp.sum(jnp.where(hit, both[0:NZ] + both[NZ:2 * NZ], 0.0), axis=0, keepdims=True)


def pick_few(heights, hot, turned, picked):
    for b in range(FEW):
        pick_block(b, heights, hot, turned, picked)
    picked[FEW:GROUPS, :] = jnp.zeros((GROUPS - FEW, BLOCK), F32)


def pick_many(heights, hot, turned, picked):
    @pl.loop(0, GROUPS)
    def _(b):
        pick_block(b, heights, hot, turned, picked)


def coefficient(table, block, j):
    return table[block * 128 + j * 32:block * 128 + (j + 1) * 32, :]


def advance(table, state, at_slots, new_state):
    own = [state[v * 32:(v + 1) * 32, :] for v in range(4)]
    slot = iota((CAP, 128), 0)
    behind = [jnp.where(slot == 0, 0.0, pltpu.roll(v, 1, 0)) for v in own]
    ahead = [jnp.where(slot == CAP - 1, 0.0, pltpu.roll(v, CAP - 1, 0)) for v in own]
    for a in range(4):
        value = coefficient(table, BASE, a) - coefficient(table, PERF, a) * at_slots
        for b in range(4):
            value = value - coefficient(table, UP + a, b) * behind[b] - coefficient(table, DOWN + a, b) * ahead[b]
        new_state[a * 32:(a + 1) * 32, :] = value


def pack_terms(order, table, state, page):
    terms = sum(coefficient(table, BACK, v) * state[v * 32:(v + 1) * 32, :] for v in range(4))
    high = terms.astype(BF16).astype(F32)
    return pack(high, terms - high, order[...], page)


def spread_block(height, high, low):
    hit = iota((NZ, BLOCK), 0) == height
    return jnp.concatenate([jnp.where(hit, high, 0.0).astype(BF16), jnp.where(hit, low, 0.0).astype(BF16)], axis=0)


def add_blocks(hot, spread):
    return lax.dot_general(hot, spread, (((1,), (1,)), ((), ())), preferred_element_type=F32)


def scatter_few(heights, hot, order, table, state, spread, page):
    high, low = pack_terms(order, table, state, page)
    for b in range(FEW):
        spread[:, b * BLOCK:(b + 1) * BLOCK] = spread_block(heights[b:b + 1, :], high[b:b + 1, :], low[b:b + 1, :])
    return add_blocks(hot[:, 0:FEW * BLOCK], spread[...])


def scatter_many(heights, hot, order, table, state, parts, wells, page):
    parts[0:GROUPS, :], parts[GROUPS:2 * GROUPS, :] = pack_terms(order, table, state, page)
    wells[...] = jnp.zeros(wells.shape, F32)

    @pl.loop(0, GROUPS)
    def _(b):
        block = spread_block(heights[pl.ds(b, 1), :], parts[pl.ds(b, 1), :], parts[pl.ds(b + GROUPS, 1), :])
        wells[...] += add_blocks(hot[:, pl.ds(pl.multiple_of(b * BLOCK, BLOCK), BLOCK)], block)


def plane_rows(x):
    return pl.ds(x * CY, CY) if isinstance(x, int) else pl.ds(pl.multiple_of(x * CY, CY), CY)


def inflow(faces, source, cells, x):
    row, depth = iota((CY, NZ), 0), iota((CY, NZ), 1)
    here = plane_rows(x)
    value = cells[here, :]
    total = source[here, :]
    if isinstance(x, int):
        if x > 0:
            total = total + faces[0, plane_rows(x - 1), :] * cells[plane_rows(x - 1), :]
        if x < CX - 1:
            total = total + faces[1, plane_rows(x + 1), :] * cells[plane_rows(x + 1), :]
    else:
        down, up = plane_rows(jnp.maximum(x - 1, 0)), plane_rows(jnp.minimum(x + 1, CX - 1))
        total = total + jnp.where(x > 0, faces[0, down, :] * cells[down, :], 0.0)
        total = total + jnp.where(x < CX - 1, faces[1, up, :] * cells[up, :], 0.0)
    total = total + jnp.where(row == 0, 0.0, pltpu.roll(faces[2, here, :] * value, 1, 0))
    total = total + jnp.where(row == CY - 1, 0.0, pltpu.roll(faces[3, here, :] * value, CY - 1, 0))
    total = total + jnp.where(depth == 0, 0.0, pltpu.roll(faces[4, here, :] * value, 1, 1))
    return total + jnp.where(depth == NZ - 1, 0.0, pltpu.roll(faces[5, here, :] * value, NZ - 1, 1))


def planes_few(wells, faces, inverse, source, cells, new_cells):
    for x in range(CX):
        here = slice(x * CY, (x + 1) * CY)
        new_cells[here, :] = inverse[here, :] * (
            inflow(faces, source, cells, x) - (wells[here, 0:NZ] + wells[here, NZ:2 * NZ]))


def planes_many(wells, faces, inverse, source, cells, new_cells):
    @pl.loop(0, CX)
    def _(x):
        here = plane_rows(x)
        added = wells[here, 0:NZ] + wells[here, NZ:2 * NZ]
        new_cells[here, :] = inverse[here, :] * (inflow(faces, source, cells, x) - added)


def sweep_kernel(counts, heights, order, hot, table, faces, inverse, source, cells, state, new_cells, new_state,
                 turned, spread, picked, page, other_page, parts, sums):
    def many():
        turn(cells, turned)
        pick_many(heights, hot, turned, picked)
        advance(table, state, unpack(picked, order, other_page), new_state)
        scatter_many(heights, hot, order, table, state, parts, sums, page)
        planes_many(sums, faces, inverse, source, cells, new_cells)

    def few():
        wells = scatter_few(heights, hot, order, table, state, spread, page)
        turn(cells, turned)
        pick_few(heights, hot, turned, picked)
        advance(table, state, unpack(picked, order, other_page), new_state)
        planes_few(wells, faces, inverse, source, cells, new_cells)

    by_number(counts, few, many)


def first_kernel(far_source, far_inverse, counts, slot_cells, *refs):
    far_out, near_out = refs[:4], refs[4:8]
    columns, heights, order, at_slots = near_out
    source, inverse, hot, turned, picked, page, semaphores = refs[8:]
    copies = bring((far_source, far_inverse), (source, inverse), semaphores)
    order[...] = owner_order(counts)
    pack_slots(slot_cells, order, columns, heights, page)
    make_hot(range(FEW), columns, hot)
    for copy in copies:
        copy.wait()
    source[...] = inverse[...] * source[...]
    turn(source, turned)

    def many():
        make_rest(columns, hot)
        pick_many(heights, hot, turned, picked)

    by_number(counts, functools.partial(pick_few, heights, hot, turned, picked), many)
    at_slots[...] = unpack(picked, order, page)
    for copy in bring(near_out, far_out, semaphores):
        copy.wait()


def second_kernel(*refs):
    far, (table, hot, source, inverse, faces, counts, heights, order, new_cells, new_state) = refs[:9], refs[9:19]
    received, at_slots, columns, spread, cells, state, page, parts, sums, semaphores = refs[19:]
    copies = bring(far, (columns, received, counts, at_slots, heights, order, source, inverse, faces), semaphores)
    copies[0].wait()
    make_hot(range(FEW), columns, hot)
    for copy in copies[1:6]:
        copy.wait()
    make_table((BASE, BACK), received, counts, table, state)
    rest = [block for block in range(BLOCKS) if block not in (BASE, BACK)]

    def cells_now():
        for copy in copies[6:]:
            copy.wait()
        cells[...] = inverse[...] * source[...]

    def many():
        make_rest(columns, hot)
        make_table(rest, received, counts, table, state)
        advance(table, state, at_slots[...], new_state)
        cells_now()
        scatter_many(heights, hot, order, table, state, parts, sums, page)
        planes_many(sums, faces, inverse, source, cells, new_cells)

    def few():
        wells = scatter_few(heights, hot, order, table, state, spread, page)
        make_table(rest, received, counts, table, state)
        advance(table, state, at_slots[...], new_state)
        cells_now()
        planes_few(wells, faces, inverse, source, cells, new_cells)

    by_number(counts, few, many)


def unpack_kernel(received, out):
    out[...] = block_transpose(received[...])


def swap(value, axis, offset):
    count = lax.axis_size(axis)
    pairs = []
    for p in range(offset, count + offset, 2):
        a, b = p % count, (p + 1) % count
        pairs += [(a, b), (b, a)]
    return lax.ppermute(value, axis, pairs)


def all_to_all(rows):
    sent = rows.reshape(128, -1)
    return lax.all_to_all(sent, AXES, split_axis=0, concat_axis=0, tiled=True).reshape(rows.shape)


def exchange(x0, x1, r0, r1):
    return swap(x0, "gx", 0), swap(x1, "gx", 1), swap(r0, AXES, 0), swap(r1, AXES, 1)


def blocks_of(array):
    lead = array.shape[0] if array.ndim == 3 else 1
    return array.reshape(lead, 4, 32, 128).transpose(0, 2, 1, 3).reshape(lead * 128, 128)


def shards(source, cell_inverse, face_coefficients, tile_counts, perf_cells, segment_kinds, segment_inverse,
           upstream_coupling, downstream_coupling, perf_to_segment, segment_to_perf, segment_source):
    source = source.reshape(COLS, NZ)
    inverse = cell_inverse.reshape(COLS, NZ)
    faces = face_coefficients.reshape(6, COLS, NZ)
    slot_cells = perf_cells.reshape(OWNERS, CAP).T
    field, planes = shape(COLS, NZ), shape(128, 128)
    rims = (shape(CY, NZ), shape(CY, NZ), shape(16, NZ), shape(16, NZ))
    turned, spread = pltpu.VMEM((2 * NZ, COLS), BF16), pltpu.VMEM((2 * NZ, FEW * BLOCK), BF16)
    picked, page = pltpu.VMEM((GROUPS, BLOCK), F32), pltpu.VMEM((OWNERS, 128), F32)
    parts, sums = pltpu.VMEM((2 * GROUPS, BLOCK), F32), pltpu.VMEM((COLS, 2 * NZ), F32)
    half = dict(flops=2 * 10**9, moved=8 * 10**6)
    whole = dict(flops=4 * 10**9, moved=16 * 10**6)

    operands = (segment_kinds.reshape(32, 128), blocks_of(segment_inverse), blocks_of(upstream_coupling),
                blocks_of(downstream_coupling), blocks_of(perf_to_segment), blocks_of(segment_to_perf),
                blocks_of(segment_source))
    packed = run(
        fold_kernel, operands, shape(BLOCKS * 128, 128), far=7, limit=56,
        scratch=[pltpu.VMEM((BLOCKS * 128, 128), F32), *(pltpu.VMEM(o.shape, o.dtype) for o in operands),
                 pltpu.SemaphoreType.DMA((7,))])
    received = all_to_all(packed)
    near_field, near_faces = pltpu.VMEM((COLS, NZ), F32), pltpu.VMEM((4, COLS, NZ), F32)
    messages = run(
        start_kernel, (source, inverse, faces), rims, far=3, limit=56,
        scratch=[near_field, near_field, near_faces, near_field, pltpu.SemaphoreType.DMA((6,))])
    messages = exchange(*messages)
    hot_shape = shape(COLS, SLOTS, dtype=BF16)
    slot_shapes = (shape(GROUPS, BLOCK, dtype=jnp.int32), shape(OWNERS, OWNERS, dtype=BF16))
    small = (shape(GROUPS, BLOCK, dtype=jnp.int32), shape(GROUPS, BLOCK, dtype=jnp.int32),
             shape(OWNERS, OWNERS, dtype=BF16), shape(CAP, 128))
    columns, heights, order, at_slots = run(
        first_kernel, (source, inverse, tile_counts, slot_cells), small, far=2, far_out=4, limit=56,
        scratch=[*(pltpu.VMEM(a.shape, a.dtype) for a in small), near_field, near_field,
                 pltpu.VMEM(hot_shape.shape, BF16), turned, picked, page, pltpu.SemaphoreType.DMA((4,))], **half)
    table, hot, source, inverse, faces, counts, heights, order, own_cells, own_state = run(
        second_kernel, (columns, received, tile_counts, at_slots, heights, order, source, inverse, faces),
        (shape(BLOCKS * 128, 128), hot_shape, field, field, shape(6, COLS, NZ), shape(1, OWNERS, dtype=jnp.int32),
         *small[1:3], field, planes), far=9,
        scratch=[pltpu.VMEM((BLOCKS * 128, 128), F32), pltpu.VMEM((CAP, 128), F32),
                 pltpu.VMEM((GROUPS, BLOCK), jnp.int32), spread, near_field,
                 pltpu.VMEM((128, 128), F32), page, parts, sums, pltpu.SemaphoreType.DMA((9,))], **half)
    for sweep in range(1, ITERS - 1):
        cells, state, *messages = run(
            functools.partial(finish_kernel, sweep == 1),
            (inverse, faces, table, own_cells, own_state, *messages), (field, planes, *rims))
        messages = exchange(*messages)
        own_cells, own_state = run(
            sweep_kernel, (counts, heights, order, hot, table, faces, inverse, source, cells, state), (field, planes),
            scratch=[turned, spread, picked, page, page, parts, sums], **whole)
    cells, packed = run(
        last_kernel, (table, own_state, *messages[2:], inverse, own_cells, *messages[:2]), (field, planes),
        scratch=[pltpu.VMEM((128, 128), F32)])
    returned = all_to_all(packed)
    states = run(unpack_kernel, (returned,), planes)
    well_adjoint = states.reshape(32, 4, 128).transpose(1, 0, 2).reshape(4, 4096)
    return cells.reshape(CX, CY, NZ), well_adjoint


def solution(mesh):
    in_specs = (
        P("gx", "gy", None),
        P("gx", "gy", None),
        P(None, "gx", "gy", None),
        P(("gx", "gy"), None),
        P(("gx", "gy"), None, None),
        P(("gx", "gy")),
        P(None, None, ("gx", "gy")),
        P(None, None, ("gx", "gy")),
        P(None, None, ("gx", "gy")),
        P(None, ("gx", "gy")),
        P(None, ("gx", "gy")),
        P(None, ("gx", "gy")),
    )
    out_specs = (P("gx", "gy", None), P(None, ("gx", "gy")))
    return jax.shard_map(shards, mesh=mesh, in_specs=in_specs, out_specs=out_specs, check_vma=False)
```

```python
import functools

import jax
import jax.numpy as jnp
from jax import lax
from jax.experimental import pallas as pl
from jax.experimental.pallas import tpu as pltpu
from jax.sharding import PartitionSpec as P

ITERS = 8
F32 = jnp.float32
BF16 = jnp.bfloat16
AXES = ("gx", "gy")
CX, CY, NZ = 8, 64, 256
COLS = CX * CY
CAP, OWNERS = 32, 128
SLOTS = CAP * OWNERS
BLOCK = 8 * CAP
GROUPS = SLOTS // BLOCK
FEW = 9
UP, DOWN, BASE, PERF, BACK, EDGE, BLOCKS = 0, 4, 8, 9, 10, 11, 12
VMEM = pl.BlockSpec(memory_space=pltpu.VMEM)
FAR = pl.BlockSpec(memory_space=pl.ANY)


def run(kernel, operands, out_shape, flops=10**6, moved=10**6, scratch=(), far=0, far_out=0, limit=28):
    many = isinstance(out_shape, (tuple, list))
    operands = [pltpu.with_memory_space_constraint(o, pltpu.HBM) if i < far else o for i, o in enumerate(operands)]
    return pl.pallas_call(
        kernel,
        out_shape=out_shape,
        in_specs=[FAR] * far + [VMEM] * (len(operands) - far),
        out_specs=tuple(FAR if i < far_out else VMEM for i in range(len(out_shape))) if many else VMEM,
        scratch_shapes=list(scratch),
        compiler_params=pltpu.CompilerParams(vmem_limit_bytes=limit * 1024 * 1024),
        cost_estimate=pl.CostEstimate(flops=flops, bytes_accessed=moved, transcendentals=0),
    )(*operands)


def bring(sources, targets, semaphores):
    copies = [pltpu.make_async_copy(a, b, semaphores.at[i]) for i, (a, b) in enumerate(zip(sources, targets))]
    for copy in copies:
        copy.start()
    return copies


def shape(*dims, dtype=F32):
    return jax.ShapeDtypeStruct(dims, dtype)


def iota(dims, axis):
    return lax.broadcasted_iota(jnp.int32, dims, axis)


def block_transpose(x):
    row = iota((128, 128), 0) & 3
    group = iota((128, 128), 1) >> 5
    y = x
    for d in range(1, 4):
        turned = jnp.where(row + d < 4, pltpu.roll(x, 128 - d, 0), pltpu.roll(x, 4 - d, 0))
        y = jnp.where(((group - row) & 3) == d, pltpu.roll(turned, 32 * d, 1), y)
    return y


def before(x):
    turned = pltpu.roll(x, 1, 1)
    return jnp.where(iota(x.shape, 1) == 0, pltpu.roll(turned, 1, 0), turned)


def after(x):
    turned = pltpu.roll(x, 127, 1)
    return jnp.where(iota(x.shape, 1) == 127, pltpu.roll(turned, x.shape[0] - 1, 0), turned)


def fold_kernel(*refs):
    far, out, table, near, semaphores = refs[:7], refs[7], refs[8], refs[9:16], refs[16]
    for copy in bring(far, near, semaphores):
        copy.wait()
    kinds, inverse, upstream, downstream, perf, back, base = near
    valid = (kinds[...] != 0).astype(F32)
    linked = (kinds[...] == 2).astype(F32)
    behind_mask = valid * before(linked)
    ahead_mask = valid * linked

    def plane(ref, a, b):
        return ref[pl.ds(a * 128 + b, 32, stride=4), :]

    def put(block, j, value):
        table[pl.ds(block * 128 + j, 32, stride=4), :] = value

    lane_slot = iota((32, 128), 1) & 31
    for a in range(4):
        row = [plane(inverse, a, c) for c in range(4)]

        def product(ref, b):
            return sum(row[c] * plane(ref, c, b) for c in range(4))

        for b in range(4):
            put(UP + a, b, behind_mask * product(upstream, b))
            put(DOWN + a, b, ahead_mask * product(downstream, b))
        start = valid * sum(row[c] * plane(base, 0, c) for c in range(4))
        put(BASE, a, start)
        put(PERF, a, valid * sum(row[c] * plane(perf, 0, c) for c in range(4)))
        put(BACK, a, plane(back, 0, a))
        put(EDGE, a, jnp.where(lane_slot == 0, before(start), after(start)))
    for block in range(BLOCKS):
        out[pl.ds(block, 128, stride=BLOCKS), :] = block_transpose(table[block * 128:(block + 1) * 128, :])


def owner_order(counts):
    active = (counts[...] > 0).astype(F32)
    earlier = (iota((OWNERS, OWNERS), 0) < iota((OWNERS, OWNERS), 1)).astype(BF16)
    place = jnp.dot(active.astype(BF16), earlier, preferred_element_type=F32).astype(jnp.int32)
    order = jnp.where((iota((OWNERS, OWNERS), 0) == place) & (active > 0.0), 1.0, 0.0)
    return order.astype(BF16)


def pack(high, low, order, page):
    both = jnp.concatenate([high, low], axis=0).astype(BF16)
    packed = lax.dot_general(both, order, (((1,), (1,)), ((), ())), preferred_element_type=F32)
    page[:, 0:2 * CAP] = packed.T
    group = iota((GROUPS, 128), 1) >> 5
    results = []
    for part in range(2):
        halves = []
        for half in range(2):
            total = None
            for g in range(4):
                rows = page[pl.ds(half * 4 + g, GROUPS, stride=8), :]
                shift = (32 * (g - part)) % 128
                rows = pltpu.roll(rows, shift, 1) if shift else rows
                total = rows if total is None else jnp.where(group == g, rows, total)
            halves.append(total)
        results.append(jnp.concatenate(halves, axis=1))
    return results


def unpack(rows, order, page):
    for q in range(8):
        part = rows[:, (q // 4) * 128:(q // 4 + 1) * 128]
        shift = (128 - 32 * (q % 4)) % 128
        page[pl.ds(q, GROUPS, stride=8), :] = pltpu.roll(part, shift, 1) if shift else part
    plane = page[...].T[0:CAP, :]
    high = plane.astype(BF16)
    both = jnp.concatenate([high, (plane - high.astype(F32)).astype(BF16)], axis=0)
    placed = jnp.dot(both, order[...], preferred_element_type=F32)
    return placed[0:CAP] + placed[CAP:2 * CAP]


def pack_slots(slot_cells, order, columns, heights, page):
    column = slot_cells[...] >> 8
    high, low = pack((column & 510).astype(F32), (column & 1).astype(F32), order[...], page)
    columns[...] = (high + low).astype(jnp.int32)
    height = (slot_cells[...] & (NZ - 1)).astype(F32)
    heights[...] = pack(height, jnp.zeros_like(height), order[...], page)[0].astype(jnp.int32)


def make_hot(blocks, columns, hot):
    index = iota((COLS, BLOCK), 0)
    for b in blocks:
        hit = index == columns[b:b + 1, :]
        hot[:, b * BLOCK:(b + 1) * BLOCK] = jnp.where(hit, 1.0, 0.0).astype(BF16)


def blocks_used(counts):
    return (jnp.sum((counts[...] > 0).astype(jnp.int32)) + 7) >> 3


def block_lanes(b):
    return pl.ds(pl.multiple_of(b * BLOCK, BLOCK), BLOCK)


def make_rest(counts, columns, hot):
    @pl.loop(FEW, blocks_used(counts))
    def _(b):
        hit = iota((COLS, BLOCK), 0) == columns[pl.ds(b, 1), :]
        hot[:, block_lanes(b)] = jnp.where(hit, 1.0, 0.0).astype(BF16)


def make_table(blocks, received, counts, table, state):
    used = ((iota((128, 128), 0) & 31) < counts[...]).astype(F32)
    for block in blocks:
        part = received[pl.ds(block, 128, stride=BLOCKS), :].T
        if block == PERF:
            part = part * used
        if block == BASE:
            state[...] = part
        table[block * 128:(block + 1) * 128, :] = part


def parity_pair(parity, upper, lower):
    even = parity == 0
    return jnp.where(even, upper, lower), jnp.where(even, lower, upper)


def emit(cells, faces, state, x0, x1, r0, r1):
    gx, gy = lax.axis_index("gx"), lax.axis_index("gy")
    last, first = pl.ds(COLS - CY, CY), pl.ds(0, CY)
    x0[...], x1[...] = parity_pair(
        gx & 1, faces[0, last, :] * cells[last, :], faces[1, first, :] * cells[first, :])
    for x in range(CX):
        top, bottom = x * CY + CY - 1, x * CY
        r0[x:x + 1, :], r1[x:x + 1, :] = parity_pair(
            gy & 1, faces[2, top:top + 1, :] * cells[top:top + 1, :],
            faces[3, bottom:bottom + 1, :] * cells[bottom:bottom + 1, :])
    if state is not None:
        for v in range(4):
            r0[8 + v:9 + v, 0:128], r1[8 + v:9 + v, 0:128] = parity_pair(
                gy & 1, state[v * 32 + 31:v * 32 + 32, :], state[v * 32:v * 32 + 1, :])
    else:
        r0[8:16, :] = jnp.zeros((8, NZ), F32)
        r1[8:16, :] = jnp.zeros((8, NZ), F32)


def start_kernel(far_source, far_inverse, far_faces, x0, x1, r0, r1, source, inverse, faces, cells, semaphores):
    top, bottom = pl.ds(COLS - CY, CY), pl.ds(0, CY)
    parts = [(0, top), (1, bottom), (2, pl.ds(0, COLS)), (3, pl.ds(0, COLS))]
    copies = bring(
        [far_source, far_inverse] + [far_faces.at[f, rows, :] for f, rows in parts],
        [source, inverse] + [faces.at[f, rows, :] for f, rows in parts], semaphores)
    for copy in copies[:2]:
        copy.wait()
    cells[...] = inverse[...] * source[...]
    for copy in copies[2:]:
        copy.wait()
    emit(cells, faces, None, x0, x1, r0, r1)


def finish_cells(inverse, cells_in, x0, x1, r0, r1, cells):
    gx, gy = lax.axis_index("gx"), lax.axis_index("gy")
    last_x, last_y = lax.axis_size("gx") - 1, lax.axis_size("gy") - 1
    cells[...] = cells_in[...]
    upper, lower = parity_pair(gx & 1, x0[...], x1[...])
    top, bottom = pl.ds(COLS - CY, CY), pl.ds(0, CY)
    cells[top, :] = cells[top, :] + inverse[top, :] * jnp.where(gx < last_x, upper, 0.0)
    cells[bottom, :] = cells[bottom, :] + inverse[bottom, :] * jnp.where(gx > 0, lower, 0.0)
    upper, lower = parity_pair(gy & 1, r0[0:8, :], r1[0:8, :])
    upper, lower = jnp.where(gy < last_y, upper, 0.0), jnp.where(gy > 0, lower, 0.0)
    for x in range(CX):
        top, bottom = pl.ds(x * CY + CY - 1, 1), pl.ds(x * CY, 1)
        cells[top, :] = cells[top, :] + inverse[top, :] * upper[x:x + 1, :]
        cells[bottom, :] = cells[bottom, :] + inverse[bottom, :] * lower[x:x + 1, :]


def finish_state(first, table, state_in, r0, r1, state):
    gy = lax.axis_index("gy")
    state[...] = state_in[...]
    if first:
        high = [table[EDGE * 128 + v * 32 + 31:EDGE * 128 + v * 32 + 32, :] for v in range(4)]
        low = [table[EDGE * 128 + v * 32:EDGE * 128 + v * 32 + 1, :] for v in range(4)]
    else:
        pairs = [parity_pair(gy & 1, r0[8 + v:9 + v, 0:128], r1[8 + v:9 + v, 0:128]) for v in range(4)]
        high, low = [p[0] for p in pairs], [p[1] for p in pairs]
    for a in range(4):
        k = a * 32
        state[k:k + 1, :] = state[k:k + 1, :] - sum(
            table[(UP + a) * 128 + b * 32:(UP + a) * 128 + b * 32 + 1, :] * low[b] for b in range(4))
        k += 31
        state[k:k + 1, :] = state[k:k + 1, :] - sum(
            table[(DOWN + a) * 128 + b * 32 + 31:(DOWN + a) * 128 + b * 32 + 32, :] * high[b] for b in range(4))


def finish_kernel(first, inverse, faces, table, cells_in, state_in, x0, x1, r0, r1, cells, state, *out):
    finish_state(first, table, state_in, r0, r1, state)
    finish_cells(inverse, cells_in, x0, x1, r0, r1, cells)
    emit(cells, faces, state, *out)


def last_kernel(table, state_in, r0, r1, inverse, cells_in, x0, x1, cells, out, state):
    finish_cells(inverse, cells_in, x0, x1, r0, r1, cells)
    finish_state(False, table, state_in, r0, r1, state)
    out[...] = state[...].T


def turn(cells, turned):
    flipped = cells[...].T
    high = flipped.astype(BF16)
    turned[0:NZ, :] = high
    turned[NZ:2 * NZ, :] = (flipped - high.astype(F32)).astype(BF16)


def pick_block(heights, hot, turned):
    both = jnp.dot(turned[...], hot, preferred_element_type=F32)
    hit = iota((NZ, BLOCK), 0) == heights
    return jnp.sum(jnp.where(hit, both[0:NZ] + both[NZ:2 * NZ], 0.0), axis=0, keepdims=True)


def pick(heights, hot, turned, picked):
    for b in range(FEW):
        picked[b:b + 1, :] = pick_block(heights[b:b + 1, :], hot[:, b * BLOCK:(b + 1) * BLOCK], turned)
    picked[FEW:GROUPS, :] = jnp.zeros((GROUPS - FEW, BLOCK), F32)


def pick_rest(counts, heights, hot, turned, picked):
    picked[...] = jnp.zeros((GROUPS, BLOCK), F32)

    @pl.loop(FEW, blocks_used(counts))
    def _(b):
        picked[pl.ds(b, 1), :] = pick_block(heights[pl.ds(b, 1), :], hot[:, block_lanes(b)], turned)


def coefficient(table, block, j):
    return table[block * 128 + j * 32:block * 128 + (j + 1) * 32, :]


def advance(table, state, at_slots, new_state):
    own = [state[v * 32:(v + 1) * 32, :] for v in range(4)]
    slot = iota((CAP, 128), 0)
    behind = [jnp.where(slot == 0, 0.0, pltpu.roll(v, 1, 0)) for v in own]
    ahead = [jnp.where(slot == CAP - 1, 0.0, pltpu.roll(v, CAP - 1, 0)) for v in own]
    for a in range(4):
        value = coefficient(table, BASE, a) - coefficient(table, PERF, a) * at_slots
        for b in range(4):
            value = value - coefficient(table, UP + a, b) * behind[b] - coefficient(table, DOWN + a, b) * ahead[b]
        new_state[a * 32:(a + 1) * 32, :] = value


def pack_terms(order, table, state, page):
    terms = sum(coefficient(table, BACK, v) * state[v * 32:(v + 1) * 32, :] for v in range(4))
    high = terms.astype(BF16).astype(F32)
    return pack(high, terms - high, order[...], page)


def spread_block(height, high, low):
    hit = iota((NZ, BLOCK), 0) == height
    return jnp.concatenate([jnp.where(hit, high, 0.0).astype(BF16), jnp.where(hit, low, 0.0).astype(BF16)], axis=0)


def add_blocks(hot, spread):
    return lax.dot_general(hot, spread, (((1,), (1,)), ((), ())), preferred_element_type=F32)


def scatter(heights, hot, order, table, state, spread, parts, page):
    high, low = pack_terms(order, table, state, page)
    parts[0:GROUPS, :], parts[GROUPS:2 * GROUPS, :] = high, low
    for b in range(FEW):
        spread[:, b * BLOCK:(b + 1) * BLOCK] = spread_block(heights[b:b + 1, :], high[b:b + 1, :], low[b:b + 1, :])
    return add_blocks(hot[:, 0:FEW * BLOCK], spread[...])


def scatter_rest(counts, heights, hot, inverse, parts, sums, new_cells):
    sums[...] = jnp.zeros(sums.shape, F32)

    @pl.loop(FEW, blocks_used(counts))
    def _(b):
        block = spread_block(heights[pl.ds(b, 1), :], parts[pl.ds(b, 1), :], parts[pl.ds(b + GROUPS, 1), :])
        sums[...] += add_blocks(hot[:, block_lanes(b)], block)

    new_cells[...] = new_cells[...] - inverse[...] * (sums[:, 0:NZ] + sums[:, NZ:2 * NZ])


def inflow(faces, source, cells, x):
    row, depth = iota((CY, NZ), 0), iota((CY, NZ), 1)
    here, down, up = (pl.ds(p * CY, CY) for p in (x, x - 1, x + 1))
    value = cells[here, :]
    total = source[here, :]
    if x > 0:
        total = total + faces[0, down, :] * cells[down, :]
    if x < CX - 1:
        total = total + faces[1, up, :] * cells[up, :]
    total = total + jnp.where(row == 0, 0.0, pltpu.roll(faces[2, here, :] * value, 1, 0))
    total = total + jnp.where(row == CY - 1, 0.0, pltpu.roll(faces[3, here, :] * value, CY - 1, 0))
    total = total + jnp.where(depth == 0, 0.0, pltpu.roll(faces[4, here, :] * value, 1, 1))
    return total + jnp.where(depth == NZ - 1, 0.0, pltpu.roll(faces[5, here, :] * value, NZ - 1, 1))


def new_planes(wells, faces, inverse, source, cells, new_cells):
    for x in range(CX):
        here = slice(x * CY, (x + 1) * CY)
        new_cells[here, :] = inverse[here, :] * (
            inflow(faces, source, cells, x) - (wells[here, 0:NZ] + wells[here, NZ:2 * NZ]))


def sweep_kernel(counts, heights, order, hot, table, faces, inverse, source, cells, state, new_cells, new_state,
                 turned, spread, picked, page, other_page, parts, sums):
    wells = scatter(heights, hot, order, table, state, spread, parts, page)
    turn(cells, turned)
    pick(heights, hot, turned, picked)
    advance(table, state, unpack(picked, order, other_page), new_state)
    new_planes(wells, faces, inverse, source, cells, new_cells)

    @pl.when(blocks_used(counts) > FEW)
    def _():
        pick_rest(counts, heights, hot, turned, picked)
        more = unpack(picked, order, page)
        for a in range(4):
            here = slice(a * 32, (a + 1) * 32)
            new_state[here, :] = new_state[here, :] - coefficient(table, PERF, a) * more
        scatter_rest(counts, heights, hot, inverse, parts, sums, new_cells)


def first_kernel(far_source, far_inverse, counts, slot_cells, *refs):
    far_out, near_out = refs[:4], refs[4:8]
    columns, heights, order, at_slots = near_out
    source, inverse, hot, turned, picked, page, semaphores = refs[8:]
    copies = bring((far_source, far_inverse), (source, inverse), semaphores)
    order[...] = owner_order(counts)
    pack_slots(slot_cells, order, columns, heights, page)
    make_hot(range(FEW), columns, hot)
    for copy in copies:
        copy.wait()
    source[...] = inverse[...] * source[...]
    turn(source, turned)
    pick(heights, hot, turned, picked)
    at_slots[...] = unpack(picked, order, page)

    @pl.when(blocks_used(counts) > FEW)
    def _():
        make_rest(counts, columns, hot)
        pick_rest(counts, heights, hot, turned, picked)
        at_slots[...] = at_slots[...] + unpack(picked, order, page)

    for copy in bring(near_out, far_out, semaphores):
        copy.wait()


def second_kernel(*refs):
    far, received, (table, hot, source, inverse, faces, counts, heights, order, new_cells, new_state) = (
        refs[:8], refs[8], refs[9:19])
    at_slots, columns, spread, cells, state, page, parts, sums, semaphores = refs[19:]
    copies = bring(far, (columns, counts, at_slots, heights, order, source, inverse, faces), semaphores)
    copies[0].wait()
    make_hot(range(FEW), columns, hot)
    for copy in copies[1:5]:
        copy.wait()
    make_table((BASE, BACK), received, counts, table, state)
    wells = scatter(heights, hot, order, table, state, spread, parts, page)
    make_table([b for b in range(BLOCKS) if b not in (BASE, BACK)], received, counts, table, state)
    advance(table, state, at_slots[...], new_state)
    for copy in copies[5:]:
        copy.wait()
    cells[...] = inverse[...] * source[...]
    new_planes(wells, faces, inverse, source, cells, new_cells)

    @pl.when(blocks_used(counts) > FEW)
    def _():
        make_rest(counts, columns, hot)
        scatter_rest(counts, heights, hot, inverse, parts, sums, new_cells)


def unpack_kernel(received, out):
    out[...] = block_transpose(received[...])


def swap(value, axis, offset):
    count = lax.axis_size(axis)
    pairs = []
    for p in range(offset, count + offset, 2):
        a, b = p % count, (p + 1) % count
        pairs += [(a, b), (b, a)]
    return lax.ppermute(value, axis, pairs)


def all_to_all(rows):
    sent = rows.reshape(128, -1)
    return lax.all_to_all(sent, AXES, split_axis=0, concat_axis=0, tiled=True).reshape(rows.shape)


def exchange(x0, x1, r0, r1):
    return swap(x0, "gx", 0), swap(x1, "gx", 1), swap(r0, AXES, 0), swap(r1, AXES, 1)


def blocks_of(array):
    lead = array.shape[0] if array.ndim == 3 else 1
    return array.reshape(lead, 4, 32, 128).transpose(0, 2, 1, 3).reshape(lead * 128, 128)


def shards(source, cell_inverse, face_coefficients, tile_counts, perf_cells, segment_kinds, segment_inverse,
           upstream_coupling, downstream_coupling, perf_to_segment, segment_to_perf, segment_source):
    source = source.reshape(COLS, NZ)
    inverse = cell_inverse.reshape(COLS, NZ)
    faces = face_coefficients.reshape(6, COLS, NZ)
    slot_cells = perf_cells.reshape(OWNERS, CAP).T
    field, planes = shape(COLS, NZ), shape(128, 128)
    rims = (shape(CY, NZ), shape(CY, NZ), shape(16, NZ), shape(16, NZ))
    turned, spread = pltpu.VMEM((2 * NZ, COLS), BF16), pltpu.VMEM((2 * NZ, FEW * BLOCK), BF16)
    picked, page = pltpu.VMEM((GROUPS, BLOCK), F32), pltpu.VMEM((OWNERS, 128), F32)
    parts, sums = pltpu.VMEM((2 * GROUPS, BLOCK), F32), pltpu.VMEM((COLS, 2 * NZ), F32)
    half = dict(flops=2 * 10**9, moved=8 * 10**6)
    whole = dict(flops=4 * 10**9, moved=16 * 10**6)

    operands = (segment_kinds.reshape(32, 128), blocks_of(segment_inverse), blocks_of(upstream_coupling),
                blocks_of(downstream_coupling), blocks_of(perf_to_segment), blocks_of(segment_to_perf),
                blocks_of(segment_source))
    packed = run(
        fold_kernel, operands, shape(BLOCKS * 128, 128), far=7, limit=56,
        scratch=[pltpu.VMEM((BLOCKS * 128, 128), F32), *(pltpu.VMEM(o.shape, o.dtype) for o in operands),
                 pltpu.SemaphoreType.DMA((7,))])
    received = all_to_all(packed)
    near_field, near_faces = pltpu.VMEM((COLS, NZ), F32), pltpu.VMEM((4, COLS, NZ), F32)
    messages = run(
        start_kernel, (source, inverse, faces), rims, far=3, limit=56,
        scratch=[near_field, near_field, near_faces, near_field, pltpu.SemaphoreType.DMA((6,))])
    messages = exchange(*messages)
    hot_shape = shape(COLS, SLOTS, dtype=BF16)
    slot_shapes = (shape(GROUPS, BLOCK, dtype=jnp.int32), shape(OWNERS, OWNERS, dtype=BF16))
    small = (shape(GROUPS, BLOCK, dtype=jnp.int32), shape(GROUPS, BLOCK, dtype=jnp.int32),
             shape(OWNERS, OWNERS, dtype=BF16), shape(CAP, 128))
    columns, heights, order, at_slots = run(
        first_kernel, (source, inverse, tile_counts, slot_cells), small, far=2, far_out=4, limit=56,
        scratch=[*(pltpu.VMEM(a.shape, a.dtype) for a in small), near_field, near_field,
                 pltpu.VMEM(hot_shape.shape, BF16), turned, picked, page, pltpu.SemaphoreType.DMA((4,))], **half)
    table, hot, source, inverse, faces, counts, heights, order, own_cells, own_state = run(
        second_kernel, (columns, tile_counts, at_slots, heights, order, source, inverse, faces, received),
        (shape(BLOCKS * 128, 128), hot_shape, field, field, shape(6, COLS, NZ), shape(1, OWNERS, dtype=jnp.int32),
         *small[1:3], field, planes), far=8,
        scratch=[pltpu.VMEM((CAP, 128), F32),
                 pltpu.VMEM((GROUPS, BLOCK), jnp.int32), spread, near_field,
                 pltpu.VMEM((128, 128), F32), page, parts, sums, pltpu.SemaphoreType.DMA((8,))], **half)
    for sweep in range(1, ITERS - 1):
        cells, state, *messages = run(
            functools.partial(finish_kernel, sweep == 1),
            (inverse, faces, table, own_cells, own_state, *messages), (field, planes, *rims))
        messages = exchange(*messages)
        own_cells, own_state = run(
            sweep_kernel, (counts, heights, order, hot, table, faces, inverse, source, cells, state), (field, planes),
            scratch=[turned, spread, picked, page, page, parts, sums], **whole)
    cells, packed = run(
        last_kernel, (table, own_state, *messages[2:], inverse, own_cells, *messages[:2]), (field, planes),
        scratch=[pltpu.VMEM((128, 128), F32)])
    returned = all_to_all(packed)
    states = run(unpack_kernel, (returned,), planes)
    well_adjoint = states.reshape(32, 4, 128).transpose(1, 0, 2).reshape(4, 4096)
    return cells.reshape(CX, CY, NZ), well_adjoint


def solution(mesh):
    in_specs = (
        P("gx", "gy", None),
        P("gx", "gy", None),
        P(None, "gx", "gy", None),
        P(("gx", "gy"), None),
        P(("gx", "gy"), None, None),
        P(("gx", "gy")),
        P(None, None, ("gx", "gy")),
        P(None, None, ("gx", "gy")),
        P(None, None, ("gx", "gy")),
        P(None, ("gx", "gy")),
        P(None, ("gx", "gy")),
        P(None, ("gx", "gy")),
    )
    out_specs = (P("gx", "gy", None), P(None, ("gx", "gy")))
    return jax.shard_map(shards, mesh=mesh, in_specs=in_specs, out_specs=out_specs, check_vma=False)
```

```python
import functools

import jax
import jax.numpy as jnp
from jax import lax
from jax.experimental import pallas as pl
from jax.experimental.pallas import tpu as pltpu
from jax.sharding import PartitionSpec as P

ITERS = 8
F32 = jnp.float32
BF16 = jnp.bfloat16
AXES = ("gx", "gy")
CX, CY, NZ = 8, 64, 256
COLS = CX * CY
CAP, OWNERS = 32, 128
SLOTS = CAP * OWNERS
BLOCK = 8 * CAP
GROUPS = SLOTS // BLOCK
FEW = 9
UP, DOWN, BASE, PERF, BACK, EDGE, BLOCKS = 0, 4, 8, 9, 10, 11, 12
VMEM = pl.BlockSpec(memory_space=pltpu.VMEM)
FAR = pl.BlockSpec(memory_space=pl.ANY)


def run(kernel, operands, out_shape, flops=10**6, moved=10**6, scratch=(), far=0, far_out=0, limit=28):
    many = isinstance(out_shape, (tuple, list))
    operands = [pltpu.with_memory_space_constraint(o, pltpu.HBM) if i < far else o for i, o in enumerate(operands)]
    return pl.pallas_call(
        kernel,
        out_shape=out_shape,
        in_specs=[FAR] * far + [VMEM] * (len(operands) - far),
        out_specs=tuple(FAR if i < far_out else VMEM for i in range(len(out_shape))) if many else VMEM,
        scratch_shapes=list(scratch),
        compiler_params=pltpu.CompilerParams(vmem_limit_bytes=limit * 1024 * 1024),
        cost_estimate=pl.CostEstimate(flops=flops, bytes_accessed=moved, transcendentals=0),
    )(*operands)


def bring(sources, targets, semaphores):
    copies = [pltpu.make_async_copy(a, b, semaphores.at[i]) for i, (a, b) in enumerate(zip(sources, targets))]
    for copy in copies:
        copy.start()
    return copies


def shape(*dims, dtype=F32):
    return jax.ShapeDtypeStruct(dims, dtype)


def iota(dims, axis):
    return lax.broadcasted_iota(jnp.int32, dims, axis)


def block_transpose(x):
    row = iota((128, 128), 0) & 3
    group = iota((128, 128), 1) >> 5
    y = x
    for d in range(1, 4):
        turned = jnp.where(row + d < 4, pltpu.roll(x, 128 - d, 0), pltpu.roll(x, 4 - d, 0))
        y = jnp.where(((group - row) & 3) == d, pltpu.roll(turned, 32 * d, 1), y)
    return y


def before(x):
    turned = pltpu.roll(x, 1, 1)
    return jnp.where(iota(x.shape, 1) == 0, pltpu.roll(turned, 1, 0), turned)


def after(x):
    turned = pltpu.roll(x, 127, 1)
    return jnp.where(iota(x.shape, 1) == 127, pltpu.roll(turned, x.shape[0] - 1, 0), turned)


def fold_kernel(*refs):
    far, out, table, near, semaphores = refs[:7], refs[7], refs[8], refs[9:16], refs[16]
    for copy in bring(far, near, semaphores):
        copy.wait()
    kinds, inverse, upstream, downstream, perf, back, base = near
    valid = (kinds[...] != 0).astype(F32)
    linked = (kinds[...] == 2).astype(F32)
    behind_mask = valid * before(linked)
    ahead_mask = valid * linked

    def plane(ref, a, b):
        return ref[pl.ds(a * 128 + b, 32, stride=4), :]

    def put(block, j, value):
        table[pl.ds(block * 128 + j, 32, stride=4), :] = value

    lane_slot = iota((32, 128), 1) & 31
    for a in range(4):
        row = [plane(inverse, a, c) for c in range(4)]

        def product(ref, b):
            return sum(row[c] * plane(ref, c, b) for c in range(4))

        for b in range(4):
            put(UP + a, b, behind_mask * product(upstream, b))
            put(DOWN + a, b, ahead_mask * product(downstream, b))
        start = valid * sum(row[c] * plane(base, 0, c) for c in range(4))
        put(BASE, a, start)
        put(PERF, a, valid * sum(row[c] * plane(perf, 0, c) for c in range(4)))
        put(BACK, a, plane(back, 0, a))
        put(EDGE, a, jnp.where(lane_slot == 0, before(start), after(start)))
    for block in range(BLOCKS):
        out[pl.ds(block, 128, stride=BLOCKS), :] = block_transpose(table[block * 128:(block + 1) * 128, :])


def owner_order(counts):
    active = (counts[...] > 0).astype(F32)
    earlier = (iota((OWNERS, OWNERS), 0) < iota((OWNERS, OWNERS), 1)).astype(BF16)
    place = jnp.dot(active.astype(BF16), earlier, preferred_element_type=F32).astype(jnp.int32)
    order = jnp.where((iota((OWNERS, OWNERS), 0) == place) & (active > 0.0), 1.0, 0.0)
    return order.astype(BF16)


def pack(high, low, order, page):
    both = jnp.concatenate([high, low], axis=0).astype(BF16)
    packed = lax.dot_general(both, order, (((1,), (1,)), ((), ())), preferred_element_type=F32)
    page[:, 0:2 * CAP] = packed.T
    group = iota((GROUPS, 128), 1) >> 5
    results = []
    for part in range(2):
        halves = []
        for half in range(2):
            total = None
            for g in range(4):
                rows = page[pl.ds(half * 4 + g, GROUPS, stride=8), :]
                shift = (32 * (g - part)) % 128
                rows = pltpu.roll(rows, shift, 1) if shift else rows
                total = rows if total is None else jnp.where(group == g, rows, total)
            halves.append(total)
        results.append(jnp.concatenate(halves, axis=1))
    return results


def unpack(rows, order, page):
    for q in range(8):
        part = rows[:, (q // 4) * 128:(q // 4 + 1) * 128]
        shift = (128 - 32 * (q % 4)) % 128
        page[pl.ds(q, GROUPS, stride=8), :] = pltpu.roll(part, shift, 1) if shift else part
    plane = page[...].T[0:CAP, :]
    high = plane.astype(BF16)
    both = jnp.concatenate([high, (plane - high.astype(F32)).astype(BF16)], axis=0)
    placed = jnp.dot(both, order[...], preferred_element_type=F32)
    return placed[0:CAP] + placed[CAP:2 * CAP]


def pack_slots(slot_cells, order, columns, heights, page):
    column = slot_cells[...] >> 8
    high, low = pack((column & 510).astype(F32), (column & 1).astype(F32), order[...], page)
    columns[...] = (high + low).astype(jnp.int32)
    height = (slot_cells[...] & (NZ - 1)).astype(F32)
    heights[...] = pack(height, jnp.zeros_like(height), order[...], page)[0].astype(jnp.int32)


def make_hot(blocks, columns, hot):
    index = iota((COLS, BLOCK), 0)
    for b in blocks:
        hit = index == columns[b:b + 1, :]
        hot[:, b * BLOCK:(b + 1) * BLOCK] = jnp.where(hit, 1.0, 0.0).astype(BF16)


def blocks_used(counts):
    return (jnp.sum((counts[...] > 0).astype(jnp.int32)) + 7) >> 3


def block_lanes(b):
    return pl.ds(pl.multiple_of(b * BLOCK, BLOCK), BLOCK)


def make_rest(counts, columns, hot):
    @pl.loop(FEW, blocks_used(counts))
    def _(b):
        hit = iota((COLS, BLOCK), 0) == columns[pl.ds(b, 1), :]
        hot[:, block_lanes(b)] = jnp.where(hit, 1.0, 0.0).astype(BF16)


def make_table(blocks, received, counts, table, state):
    used = ((iota((128, 128), 0) & 31) < counts[...]).astype(F32)
    for block in blocks:
        part = received[pl.ds(block, 128, stride=BLOCKS), :].T
        if block == PERF:
            part = part * used
        if block == BASE:
            state[...] = part
        table[block * 128:(block + 1) * 128, :] = part


def parity_pair(parity, upper, lower):
    even = parity == 0
    return jnp.where(even, upper, lower), jnp.where(even, lower, upper)


def emit(cells, faces, state, x0, x1, r0, r1):
    gx, gy = lax.axis_index("gx"), lax.axis_index("gy")
    last, first = pl.ds(COLS - CY, CY), pl.ds(0, CY)
    x0[...], x1[...] = parity_pair(
        gx & 1, faces[0, last, :] * cells[last, :], faces[1, first, :] * cells[first, :])
    for x in range(CX):
        top, bottom = x * CY + CY - 1, x * CY
        r0[x:x + 1, :], r1[x:x + 1, :] = parity_pair(
            gy & 1, faces[2, top:top + 1, :] * cells[top:top + 1, :],
            faces[3, bottom:bottom + 1, :] * cells[bottom:bottom + 1, :])
    if state is not None:
        for v in range(4):
            r0[8 + v:9 + v, 0:128], r1[8 + v:9 + v, 0:128] = parity_pair(
                gy & 1, state[v * 32 + 31:v * 32 + 32, :], state[v * 32:v * 32 + 1, :])
    else:
        r0[8:16, :] = jnp.zeros((8, NZ), F32)
        r1[8:16, :] = jnp.zeros((8, NZ), F32)


def start_kernel(far_source, far_inverse, far_faces, x0, x1, r0, r1, source, inverse, faces, cells, semaphores):
    top, bottom = pl.ds(COLS - CY, CY), pl.ds(0, CY)
    parts = [(0, top), (1, bottom), (2, pl.ds(0, COLS)), (3, pl.ds(0, COLS))]
    copies = bring(
        [far_source, far_inverse] + [far_faces.at[f, rows, :] for f, rows in parts],
        [source, inverse] + [faces.at[f, rows, :] for f, rows in parts], semaphores)
    for copy in copies[:2]:
        copy.wait()
    cells[...] = inverse[...] * source[...]
    for copy in copies[2:]:
        copy.wait()
    emit(cells, faces, None, x0, x1, r0, r1)


def finish_cells(inverse, cells_in, x0, x1, r0, r1, cells):
    gx, gy = lax.axis_index("gx"), lax.axis_index("gy")
    last_x, last_y = lax.axis_size("gx") - 1, lax.axis_size("gy") - 1
    cells[...] = cells_in[...]
    upper, lower = parity_pair(gx & 1, x0[...], x1[...])
    top, bottom = pl.ds(COLS - CY, CY), pl.ds(0, CY)
    cells[top, :] = cells[top, :] + inverse[top, :] * jnp.where(gx < last_x, upper, 0.0)
    cells[bottom, :] = cells[bottom, :] + inverse[bottom, :] * jnp.where(gx > 0, lower, 0.0)
    upper, lower = parity_pair(gy & 1, r0[0:8, :], r1[0:8, :])
    upper, lower = jnp.where(gy < last_y, upper, 0.0), jnp.where(gy > 0, lower, 0.0)
    for x in range(CX):
        top, bottom = pl.ds(x * CY + CY - 1, 1), pl.ds(x * CY, 1)
        cells[top, :] = cells[top, :] + inverse[top, :] * upper[x:x + 1, :]
        cells[bottom, :] = cells[bottom, :] + inverse[bottom, :] * lower[x:x + 1, :]


def finish_state(first, table, state_in, r0, r1, state):
    gy = lax.axis_index("gy")
    state[...] = state_in[...]
    if first:
        high = [table[EDGE * 128 + v * 32 + 31:EDGE * 128 + v * 32 + 32, :] for v in range(4)]
        low = [table[EDGE * 128 + v * 32:EDGE * 128 + v * 32 + 1, :] for v in range(4)]
    else:
        pairs = [parity_pair(gy & 1, r0[8 + v:9 + v, 0:128], r1[8 + v:9 + v, 0:128]) for v in range(4)]
        high, low = [p[0] for p in pairs], [p[1] for p in pairs]
    for a in range(4):
        k = a * 32
        state[k:k + 1, :] = state[k:k + 1, :] - sum(
            table[(UP + a) * 128 + b * 32:(UP + a) * 128 + b * 32 + 1, :] * low[b] for b in range(4))
        k += 31
        state[k:k + 1, :] = state[k:k + 1, :] - sum(
            table[(DOWN + a) * 128 + b * 32 + 31:(DOWN + a) * 128 + b * 32 + 32, :] * high[b] for b in range(4))


def finish_kernel(first, inverse, faces, table, cells_in, state_in, x1, r1, x0, r0, cells, state, *out):
    finish_state(first, table, state_in, r0, r1, state)
    finish_cells(inverse, cells_in, x0, x1, r0, r1, cells)
    emit(cells, faces, state, *out)


def last_kernel(table, state_in, inverse, cells_in, x1, r1, x0, r0, cells, out, state):
    finish_cells(inverse, cells_in, x0, x1, r0, r1, cells)
    finish_state(False, table, state_in, r0, r1, state)
    out[...] = state[...].T


def turn(cells, turned):
    flipped = cells[...].T
    high = flipped.astype(BF16)
    turned[0:NZ, :] = high
    turned[NZ:2 * NZ, :] = (flipped - high.astype(F32)).astype(BF16)


def pick_block(heights, hot, turned):
    both = jnp.dot(turned[...], hot, preferred_element_type=F32)
    hit = iota((NZ, BLOCK), 0) == heights
    return jnp.sum(jnp.where(hit, both[0:NZ] + both[NZ:2 * NZ], 0.0), axis=0, keepdims=True)


def pick(heights, hot, turned, picked):
    for b in range(FEW):
        picked[b:b + 1, :] = pick_block(heights[b:b + 1, :], hot[:, b * BLOCK:(b + 1) * BLOCK], turned)
    picked[FEW:GROUPS, :] = jnp.zeros((GROUPS - FEW, BLOCK), F32)


def pick_rest(counts, heights, hot, turned, picked):
    picked[...] = jnp.zeros((GROUPS, BLOCK), F32)

    @pl.loop(FEW, blocks_used(counts))
    def _(b):
        picked[pl.ds(b, 1), :] = pick_block(heights[pl.ds(b, 1), :], hot[:, block_lanes(b)], turned)


def coefficient(table, block, j):
    return table[block * 128 + j * 32:block * 128 + (j + 1) * 32, :]


def advance(table, state, at_slots, new_state):
    own = [state[v * 32:(v + 1) * 32, :] for v in range(4)]
    slot = iota((CAP, 128), 0)
    behind = [jnp.where(slot == 0, 0.0, pltpu.roll(v, 1, 0)) for v in own]
    ahead = [jnp.where(slot == CAP - 1, 0.0, pltpu.roll(v, CAP - 1, 0)) for v in own]
    for a in range(4):
        value = coefficient(table, BASE, a) - coefficient(table, PERF, a) * at_slots
        for b in range(4):
            value = value - coefficient(table, UP + a, b) * behind[b] - coefficient(table, DOWN + a, b) * ahead[b]
        new_state[a * 32:(a + 1) * 32, :] = value


def pack_terms(order, table, state, page):
    terms = sum(coefficient(table, BACK, v) * state[v * 32:(v + 1) * 32, :] for v in range(4))
    high = terms.astype(BF16).astype(F32)
    return pack(high, terms - high, order[...], page)


def spread_block(height, high, low):
    hit = iota((NZ, BLOCK), 0) == height
    return jnp.concatenate([jnp.where(hit, high, 0.0).astype(BF16), jnp.where(hit, low, 0.0).astype(BF16)], axis=0)


def add_blocks(hot, spread):
    return lax.dot_general(hot, spread, (((1,), (1,)), ((), ())), preferred_element_type=F32)


def scatter(heights, hot, order, table, state, spread, parts, page):
    high, low = pack_terms(order, table, state, page)
    parts[0:GROUPS, :], parts[GROUPS:2 * GROUPS, :] = high, low
    for b in range(FEW):
        spread[:, b * BLOCK:(b + 1) * BLOCK] = spread_block(heights[b:b + 1, :], high[b:b + 1, :], low[b:b + 1, :])
    return add_blocks(hot[:, 0:FEW * BLOCK], spread[...])


def scatter_rest(counts, heights, hot, inverse, parts, sums, new_cells):
    sums[...] = jnp.zeros(sums.shape, F32)

    @pl.loop(FEW, blocks_used(counts))
    def _(b):
        block = spread_block(heights[pl.ds(b, 1), :], parts[pl.ds(b, 1), :], parts[pl.ds(b + GROUPS, 1), :])
        sums[...] += add_blocks(hot[:, block_lanes(b)], block)

    new_cells[...] = new_cells[...] - inverse[...] * (sums[:, 0:NZ] + sums[:, NZ:2 * NZ])


def inflow(faces, source, cells, x):
    row, depth = iota((CY, NZ), 0), iota((CY, NZ), 1)
    here, down, up = (pl.ds(p * CY, CY) for p in (x, x - 1, x + 1))
    value = cells[here, :]
    total = source[here, :]
    if x > 0:
        total = total + faces[0, down, :] * cells[down, :]
    if x < CX - 1:
        total = total + faces[1, up, :] * cells[up, :]
    total = total + jnp.where(row == 0, 0.0, pltpu.roll(faces[2, here, :] * value, 1, 0))
    total = total + jnp.where(row == CY - 1, 0.0, pltpu.roll(faces[3, here, :] * value, CY - 1, 0))
    total = total + jnp.where(depth == 0, 0.0, pltpu.roll(faces[4, here, :] * value, 1, 1))
    return total + jnp.where(depth == NZ - 1, 0.0, pltpu.roll(faces[5, here, :] * value, NZ - 1, 1))


def new_planes(wells, faces, inverse, source, cells, new_cells):
    for x in range(CX):
        here = slice(x * CY, (x + 1) * CY)
        new_cells[here, :] = inverse[here, :] * (
            inflow(faces, source, cells, x) - (wells[here, 0:NZ] + wells[here, NZ:2 * NZ]))


def sweep_kernel(counts, heights, order, hot, table, faces, inverse, source, cells, state, new_cells, new_state,
                 turned, spread, picked, page, other_page, parts, sums):
    wells = scatter(heights, hot, order, table, state, spread, parts, page)
    turn(cells, turned)
    pick(heights, hot, turned, picked)
    advance(table, state, unpack(picked, order, other_page), new_state)
    new_planes(wells, faces, inverse, source, cells, new_cells)

    @pl.when(blocks_used(counts) > FEW)
    def _():
        pick_rest(counts, heights, hot, turned, picked)
        more = unpack(picked, order, page)
        for a in range(4):
            here = slice(a * 32, (a + 1) * 32)
            new_state[here, :] = new_state[here, :] - coefficient(table, PERF, a) * more
        scatter_rest(counts, heights, hot, inverse, parts, sums, new_cells)


def first_kernel(far_source, far_inverse, counts, slot_cells, *refs):
    far_out, near_out = refs[:4], refs[4:8]
    columns, heights, order, at_slots = near_out
    source, inverse, hot, turned, picked, page, semaphores = refs[8:]
    copies = bring((far_source, far_inverse), (source, inverse), semaphores)
    order[...] = owner_order(counts)
    pack_slots(slot_cells, order, columns, heights, page)
    make_hot(range(FEW), columns, hot)
    for copy in copies:
        copy.wait()
    source[...] = inverse[...] * source[...]
    turn(source, turned)
    pick(heights, hot, turned, picked)
    at_slots[...] = unpack(picked, order, page)

    @pl.when(blocks_used(counts) > FEW)
    def _():
        make_rest(counts, columns, hot)
        pick_rest(counts, heights, hot, turned, picked)
        at_slots[...] = at_slots[...] + unpack(picked, order, page)

    for copy in bring(near_out, far_out, semaphores):
        copy.wait()


def second_kernel(*refs):
    far, received, (table, hot, source, inverse, faces, counts, heights, order, new_cells, new_state) = (
        refs[:8], refs[8], refs[9:19])
    at_slots, columns, spread, cells, state, page, parts, sums, semaphores = refs[19:]
    copies = bring(far, (columns, counts, at_slots, heights, order, source, inverse, faces), semaphores)
    copies[0].wait()
    make_hot(range(FEW), columns, hot)
    for copy in copies[1:5]:
        copy.wait()
    make_table((BASE, BACK), received, counts, table, state)
    wells = scatter(heights, hot, order, table, state, spread, parts, page)
    make_table([b for b in range(BLOCKS) if b not in (BASE, BACK)], received, counts, table, state)
    advance(table, state, at_slots[...], new_state)
    for copy in copies[5:]:
        copy.wait()
    cells[...] = inverse[...] * source[...]
    new_planes(wells, faces, inverse, source, cells, new_cells)

    @pl.when(blocks_used(counts) > FEW)
    def _():
        make_rest(counts, columns, hot)
        scatter_rest(counts, heights, hot, inverse, parts, sums, new_cells)


def unpack_kernel(received, out):
    out[...] = block_transpose(received[...])


def swap(value, axis, offset):
    count = lax.axis_size(axis)
    pairs = []
    for p in range(offset, count + offset, 2):
        a, b = p % count, (p + 1) % count
        pairs += [(a, b), (b, a)]
    return lax.ppermute(value, axis, pairs)


def all_to_all(rows):
    sent = rows.reshape(128, -1)
    return lax.all_to_all(sent, AXES, split_axis=0, concat_axis=0, tiled=True).reshape(rows.shape)


def exchange(x0, x1, r0, r1):
    return swap(x1, "gx", 1), swap(r1, AXES, 1), swap(x0, "gx", 0), swap(r0, AXES, 0)


def blocks_of(array):
    lead = array.shape[0] if array.ndim == 3 else 1
    return array.reshape(lead, 4, 32, 128).transpose(0, 2, 1, 3).reshape(lead * 128, 128)


def shards(source, cell_inverse, face_coefficients, tile_counts, perf_cells, segment_kinds, segment_inverse,
           upstream_coupling, downstream_coupling, perf_to_segment, segment_to_perf, segment_source):
    source = source.reshape(COLS, NZ)
    inverse = cell_inverse.reshape(COLS, NZ)
    faces = face_coefficients.reshape(6, COLS, NZ)
    slot_cells = perf_cells.reshape(OWNERS, CAP).T
    field, planes = shape(COLS, NZ), shape(128, 128)
    rims = (shape(CY, NZ), shape(CY, NZ), shape(16, NZ), shape(16, NZ))
    turned, spread = pltpu.VMEM((2 * NZ, COLS), BF16), pltpu.VMEM((2 * NZ, FEW * BLOCK), BF16)
    picked, page = pltpu.VMEM((GROUPS, BLOCK), F32), pltpu.VMEM((OWNERS, 128), F32)
    parts, sums = pltpu.VMEM((2 * GROUPS, BLOCK), F32), pltpu.VMEM((COLS, 2 * NZ), F32)
    half = dict(flops=2 * 10**9, moved=8 * 10**6)
    whole = dict(flops=4 * 10**9, moved=16 * 10**6)

    operands = (segment_kinds.reshape(32, 128), blocks_of(segment_inverse), blocks_of(upstream_coupling),
                blocks_of(downstream_coupling), blocks_of(perf_to_segment), blocks_of(segment_to_perf),
                blocks_of(segment_source))
    packed = run(
        fold_kernel, operands, shape(BLOCKS * 128, 128), far=7, limit=56,
        scratch=[pltpu.VMEM((BLOCKS * 128, 128), F32), *(pltpu.VMEM(o.shape, o.dtype) for o in operands),
                 pltpu.SemaphoreType.DMA((7,))])
    received = all_to_all(packed)
    near_field, near_faces = pltpu.VMEM((COLS, NZ), F32), pltpu.VMEM((4, COLS, NZ), F32)
    messages = run(
        start_kernel, (source, inverse, faces), rims, far=3, limit=56,
        scratch=[near_field, near_field, near_faces, near_field, pltpu.SemaphoreType.DMA((6,))])
    messages = exchange(*messages)
    hot_shape = shape(COLS, SLOTS, dtype=BF16)
    slot_shapes = (shape(GROUPS, BLOCK, dtype=jnp.int32), shape(OWNERS, OWNERS, dtype=BF16))
    small = (shape(GROUPS, BLOCK, dtype=jnp.int32), shape(GROUPS, BLOCK, dtype=jnp.int32),
             shape(OWNERS, OWNERS, dtype=BF16), shape(CAP, 128))
    columns, heights, order, at_slots = run(
        first_kernel, (source, inverse, tile_counts, slot_cells), small, far=2, far_out=4, limit=56,
        scratch=[*(pltpu.VMEM(a.shape, a.dtype) for a in small), near_field, near_field,
                 pltpu.VMEM(hot_shape.shape, BF16), turned, picked, page, pltpu.SemaphoreType.DMA((4,))], **half)
    table, hot, source, inverse, faces, counts, heights, order, own_cells, own_state = run(
        second_kernel, (columns, tile_counts, at_slots, heights, order, source, inverse, faces, received),
        (shape(BLOCKS * 128, 128), hot_shape, field, field, shape(6, COLS, NZ), shape(1, OWNERS, dtype=jnp.int32),
         *small[1:3], field, planes), far=8,
        scratch=[pltpu.VMEM((CAP, 128), F32),
                 pltpu.VMEM((GROUPS, BLOCK), jnp.int32), spread, near_field,
                 pltpu.VMEM((128, 128), F32), page, parts, sums, pltpu.SemaphoreType.DMA((8,))], **half)
    for sweep in range(1, ITERS - 1):
        cells, state, *messages = run(
            functools.partial(finish_kernel, sweep == 1),
            (inverse, faces, table, own_cells, own_state, *messages), (field, planes, *rims))
        messages = exchange(*messages)
        own_cells, own_state = run(
            sweep_kernel, (counts, heights, order, hot, table, faces, inverse, source, cells, state), (field, planes),
            scratch=[turned, spread, picked, page, page, parts, sums], **whole)
    cells, packed = run(
        last_kernel, (table, own_state, inverse, own_cells, *messages), (field, planes),
        scratch=[pltpu.VMEM((128, 128), F32)])
    returned = all_to_all(packed)
    states = run(unpack_kernel, (returned,), planes)
    well_adjoint = states.reshape(32, 4, 128).transpose(1, 0, 2).reshape(4, 4096)
    return cells.reshape(CX, CY, NZ), well_adjoint


def solution(mesh):
    in_specs = (
        P("gx", "gy", None),
        P("gx", "gy", None),
        P(None, "gx", "gy", None),
        P(("gx", "gy"), None),
        P(("gx", "gy"), None, None),
        P(("gx", "gy")),
        P(None, None, ("gx", "gy")),
        P(None, None, ("gx", "gy")),
        P(None, None, ("gx", "gy")),
        P(None, ("gx", "gy")),
        P(None, ("gx", "gy")),
        P(None, ("gx", "gy")),
    )
    out_specs = (P("gx", "gy", None), P(None, ("gx", "gy")))
    return jax.shard_map(shards, mesh=mesh, in_specs=in_specs, out_specs=out_specs, check_vma=False)
```

```python
import functools

import jax
import jax.numpy as jnp
from jax import lax
from jax.experimental import pallas as pl
from jax.experimental.pallas import tpu as pltpu
from jax.sharding import PartitionSpec as P

ITERS = 8
F32 = jnp.float32
BF16 = jnp.bfloat16
AXES = ("gx", "gy")
CX, CY, NZ = 8, 64, 256
COLS = CX * CY
CAP, OWNERS = 32, 128
SLOTS = CAP * OWNERS
BLOCK = 8 * CAP
GROUPS = SLOTS // BLOCK
FEW = 9
UP, DOWN, BASE, PERF, BACK, EDGE, BLOCKS = 0, 4, 8, 9, 10, 11, 12
VMEM = pl.BlockSpec(memory_space=pltpu.VMEM)
FAR = pl.BlockSpec(memory_space=pl.ANY)


def run(kernel, operands, out_shape, flops=10**6, moved=10**6, scratch=(), far=0, far_out=0, limit=28):
    many = isinstance(out_shape, (tuple, list))
    operands = [pltpu.with_memory_space_constraint(o, pltpu.HBM) if i < far else o for i, o in enumerate(operands)]
    return pl.pallas_call(
        kernel,
        out_shape=out_shape,
        in_specs=[FAR] * far + [VMEM] * (len(operands) - far),
        out_specs=tuple(FAR if i < far_out else VMEM for i in range(len(out_shape))) if many else VMEM,
        scratch_shapes=list(scratch),
        compiler_params=pltpu.CompilerParams(vmem_limit_bytes=limit * 1024 * 1024),
        cost_estimate=pl.CostEstimate(flops=flops, bytes_accessed=moved, transcendentals=0),
    )(*operands)


def bring(sources, targets, semaphores):
    copies = [pltpu.make_async_copy(a, b, semaphores.at[i]) for i, (a, b) in enumerate(zip(sources, targets))]
    for copy in copies:
        copy.start()
    return copies


def shape(*dims, dtype=F32):
    return jax.ShapeDtypeStruct(dims, dtype)


def iota(dims, axis):
    return lax.broadcasted_iota(jnp.int32, dims, axis)


def block_transpose(x):
    row = iota((128, 128), 0) & 3
    group = iota((128, 128), 1) >> 5
    y = x
    for d in range(1, 4):
        turned = jnp.where(row + d < 4, pltpu.roll(x, 128 - d, 0), pltpu.roll(x, 4 - d, 0))
        y = jnp.where(((group - row) & 3) == d, pltpu.roll(turned, 32 * d, 1), y)
    return y


def before(x):
    turned = pltpu.roll(x, 1, 1)
    return jnp.where(iota(x.shape, 1) == 0, pltpu.roll(turned, 1, 0), turned)


def after(x):
    turned = pltpu.roll(x, 127, 1)
    return jnp.where(iota(x.shape, 1) == 127, pltpu.roll(turned, x.shape[0] - 1, 0), turned)


def fold_kernel(*refs):
    far, out, table, near, semaphores = refs[:7], refs[7], refs[8], refs[9:16], refs[16]
    copies = bring(far, near, semaphores)
    kinds, inverse, base, perf, back, upstream, downstream = near
    for copy in copies[:5]:
        copy.wait()
    valid = (kinds[...] != 0).astype(F32)
    linked = (kinds[...] == 2).astype(F32)

    def plane(ref, a, b):
        return ref[pl.ds(a * 128 + b, 32, stride=4), :]

    def put(block, j, value):
        table[pl.ds(block * 128 + j, 32, stride=4), :] = value

    def finish(blocks):
        for block in blocks:
            out[pl.ds(block, 128, stride=BLOCKS), :] = block_transpose(table[block * 128:(block + 1) * 128, :])

    lane_slot = iota((32, 128), 1) & 31
    for a in range(4):
        row = [plane(inverse, a, c) for c in range(4)]
        start = valid * sum(row[c] * plane(base, 0, c) for c in range(4))
        put(BASE, a, start)
        put(PERF, a, valid * sum(row[c] * plane(perf, 0, c) for c in range(4)))
        put(BACK, a, plane(back, 0, a))
        put(EDGE, a, jnp.where(lane_slot == 0, before(start), after(start)))
    finish((BASE, PERF, BACK, EDGE))
    for block, mask, ref, copy in ((UP, valid * before(linked), upstream, copies[5]),
                                   (DOWN, valid * linked, downstream, copies[6])):
        copy.wait()
        for a in range(4):
            row = [mask * plane(inverse, a, c) for c in range(4)]
            for b in range(4):
                put(block + a, b, sum(row[c] * plane(ref, c, b) for c in range(4)))
        finish(range(block, block + 4))


def owner_order(counts):
    active = (counts[...] > 0).astype(F32)
    earlier = (iota((OWNERS, OWNERS), 0) < iota((OWNERS, OWNERS), 1)).astype(BF16)
    place = jnp.dot(active.astype(BF16), earlier, preferred_element_type=F32).astype(jnp.int32)
    order = jnp.where((iota((OWNERS, OWNERS), 0) == place) & (active > 0.0), 1.0, 0.0)
    return order.astype(BF16)


def pack(high, low, order, page):
    both = jnp.concatenate([high, low], axis=0).astype(BF16)
    packed = lax.dot_general(both, order, (((1,), (1,)), ((), ())), preferred_element_type=F32)
    page[:, 0:2 * CAP] = packed.T
    group = iota((GROUPS, 128), 1) >> 5
    results = []
    for part in range(2):
        halves = []
        for half in range(2):
            total = None
            for g in range(4):
                rows = page[pl.ds(half * 4 + g, GROUPS, stride=8), :]
                shift = (32 * (g - part)) % 128
                rows = pltpu.roll(rows, shift, 1) if shift else rows
                total = rows if total is None else jnp.where(group == g, rows, total)
            halves.append(total)
        results.append(jnp.concatenate(halves, axis=1))
    return results


def unpack(rows, order, page):
    for q in range(8):
        part = rows[:, (q // 4) * 128:(q // 4 + 1) * 128]
        shift = (128 - 32 * (q % 4)) % 128
        page[pl.ds(q, GROUPS, stride=8), :] = pltpu.roll(part, shift, 1) if shift else part
    plane = page[...].T[0:CAP, :]
    high = plane.astype(BF16)
    both = jnp.concatenate([high, (plane - high.astype(F32)).astype(BF16)], axis=0)
    placed = jnp.dot(both, order[...], preferred_element_type=F32)
    return placed[0:CAP] + placed[CAP:2 * CAP]


def pack_slots(slot_cells, order, columns, heights, page):
    column = slot_cells[...] >> 8
    high, low = pack((column & 510).astype(F32), (column & 1).astype(F32), order[...], page)
    columns[...] = (high + low).astype(jnp.int32)
    height = (slot_cells[...] & (NZ - 1)).astype(F32)
    heights[...] = pack(height, jnp.zeros_like(height), order[...], page)[0].astype(jnp.int32)


def make_hot(blocks, columns, hot):
    index = iota((COLS, BLOCK), 0)
    for b in blocks:
        hit = index == columns[b:b + 1, :]
        hot[:, b * BLOCK:(b + 1) * BLOCK] = jnp.where(hit, 1.0, 0.0).astype(BF16)


def blocks_used(counts):
    return (jnp.sum((counts[...] > 0).astype(jnp.int32)) + 7) >> 3


def block_lanes(b):
    return pl.ds(pl.multiple_of(b * BLOCK, BLOCK), BLOCK)


def make_rest(counts, columns, hot):
    @pl.loop(FEW, blocks_used(counts))
    def _(b):
        hit = iota((COLS, BLOCK), 0) == columns[pl.ds(b, 1), :]
        hot[:, block_lanes(b)] = jnp.where(hit, 1.0, 0.0).astype(BF16)


def make_table(blocks, received, counts, table, state):
    used = ((iota((128, 128), 0) & 31) < counts[...]).astype(F32)
    for block in blocks:
        part = received[pl.ds(block, 128, stride=BLOCKS), :].T
        if block == PERF:
            part = part * used
        if block == BASE:
            state[...] = part
        table[block * 128:(block + 1) * 128, :] = part


def parity_pair(parity, upper, lower):
    even = parity == 0
    return jnp.where(even, upper, lower), jnp.where(even, lower, upper)


def emit(cells, faces, state, x0, x1, r0, r1):
    gx, gy = lax.axis_index("gx"), lax.axis_index("gy")
    last, first = pl.ds(COLS - CY, CY), pl.ds(0, CY)
    x0[...], x1[...] = parity_pair(
        gx & 1, faces[0, last, :] * cells[last, :], faces[1, first, :] * cells[first, :])
    for x in range(CX):
        top, bottom = x * CY + CY - 1, x * CY
        r0[x:x + 1, :], r1[x:x + 1, :] = parity_pair(
            gy & 1, faces[2, top:top + 1, :] * cells[top:top + 1, :],
            faces[3, bottom:bottom + 1, :] * cells[bottom:bottom + 1, :])
    if state is not None:
        for v in range(4):
            r0[8 + v:9 + v, 0:128], r1[8 + v:9 + v, 0:128] = parity_pair(
                gy & 1, state[v * 32 + 31:v * 32 + 32, :], state[v * 32:v * 32 + 1, :])
    else:
        r0[8:16, :] = jnp.zeros((8, NZ), F32)
        r1[8:16, :] = jnp.zeros((8, NZ), F32)


def start_kernel(far_source, far_inverse, far_faces, x0, x1, r0, r1, source, inverse, faces, cells, semaphores):
    top, bottom = pl.ds(COLS - CY, CY), pl.ds(0, CY)
    parts = [(0, top), (1, bottom), (2, pl.ds(0, COLS)), (3, pl.ds(0, COLS))]
    copies = bring(
        [far_source, far_inverse] + [far_faces.at[f, rows, :] for f, rows in parts],
        [source, inverse] + [faces.at[f, rows, :] for f, rows in parts], semaphores)
    for copy in copies[:2]:
        copy.wait()
    cells[...] = inverse[...] * source[...]
    for copy in copies[2:]:
        copy.wait()
    emit(cells, faces, None, x0, x1, r0, r1)


def finish_cells(inverse, cells_in, x0, x1, r0, r1, cells):
    gx, gy = lax.axis_index("gx"), lax.axis_index("gy")
    last_x, last_y = lax.axis_size("gx") - 1, lax.axis_size("gy") - 1
    cells[...] = cells_in[...]
    upper, lower = parity_pair(gx & 1, x0[...], x1[...])
    top, bottom = pl.ds(COLS - CY, CY), pl.ds(0, CY)
    cells[top, :] = cells[top, :] + inverse[top, :] * jnp.where(gx < last_x, upper, 0.0)
    cells[bottom, :] = cells[bottom, :] + inverse[bottom, :] * jnp.where(gx > 0, lower, 0.0)
    upper, lower = parity_pair(gy & 1, r0[0:8, :], r1[0:8, :])
    upper, lower = jnp.where(gy < last_y, upper, 0.0), jnp.where(gy > 0, lower, 0.0)
    for x in range(CX):
        top, bottom = pl.ds(x * CY + CY - 1, 1), pl.ds(x * CY, 1)
        cells[top, :] = cells[top, :] + inverse[top, :] * upper[x:x + 1, :]
        cells[bottom, :] = cells[bottom, :] + inverse[bottom, :] * lower[x:x + 1, :]


def finish_state(first, table, state_in, r0, r1, state):
    gy = lax.axis_index("gy")
    state[...] = state_in[...]
    if first:
        high = [table[EDGE * 128 + v * 32 + 31:EDGE * 128 + v * 32 + 32, :] for v in range(4)]
        low = [table[EDGE * 128 + v * 32:EDGE * 128 + v * 32 + 1, :] for v in range(4)]
    else:
        pairs = [parity_pair(gy & 1, r0[8 + v:9 + v, 0:128], r1[8 + v:9 + v, 0:128]) for v in range(4)]
        high, low = [p[0] for p in pairs], [p[1] for p in pairs]
    for a in range(4):
        k = a * 32
        state[k:k + 1, :] = state[k:k + 1, :] - sum(
            table[(UP + a) * 128 + b * 32:(UP + a) * 128 + b * 32 + 1, :] * low[b] for b in range(4))
        k += 31
        state[k:k + 1, :] = state[k:k + 1, :] - sum(
            table[(DOWN + a) * 128 + b * 32 + 31:(DOWN + a) * 128 + b * 32 + 32, :] * high[b] for b in range(4))


def finish_kernel(first, inverse, faces, table, cells_in, state_in, x1, r1, x0, r0, cells, state, *out):
    finish_state(first, table, state_in, r0, r1, state)
    finish_cells(inverse, cells_in, x0, x1, r0, r1, cells)
    emit(cells, faces, state, *out)


def last_kernel(table, state_in, inverse, cells_in, x1, r1, x0, r0, far_cells, out, cells, state, semaphore):
    finish_cells(inverse, cells_in, x0, x1, r0, r1, cells)
    (copy,) = bring((cells,), (far_cells,), semaphore)
    finish_state(False, table, state_in, r0, r1, state)
    out[...] = state[...].T
    copy.wait()


def turn(cells, turned):
    flipped = cells[...].T
    high = flipped.astype(BF16)
    turned[0:NZ, :] = high
    turned[NZ:2 * NZ, :] = (flipped - high.astype(F32)).astype(BF16)


def pick_block(heights, hot, turned):
    both = jnp.dot(turned[...], hot, preferred_element_type=F32)
    hit = iota((NZ, BLOCK), 0) == heights
    return jnp.sum(jnp.where(hit, both[0:NZ] + both[NZ:2 * NZ], 0.0), axis=0, keepdims=True)


def pick(heights, hot, turned, picked):
    for b in range(FEW):
        picked[b:b + 1, :] = pick_block(heights[b:b + 1, :], hot[:, b * BLOCK:(b + 1) * BLOCK], turned)
    picked[FEW:GROUPS, :] = jnp.zeros((GROUPS - FEW, BLOCK), F32)


def pick_rest(counts, heights, hot, turned, picked):
    picked[...] = jnp.zeros((GROUPS, BLOCK), F32)

    @pl.loop(FEW, blocks_used(counts))
    def _(b):
        picked[pl.ds(b, 1), :] = pick_block(heights[pl.ds(b, 1), :], hot[:, block_lanes(b)], turned)


def coefficient(table, block, j):
    return table[block * 128 + j * 32:block * 128 + (j + 1) * 32, :]


def advance(table, state, at_slots, new_state):
    own = [state[v * 32:(v + 1) * 32, :] for v in range(4)]
    slot = iota((CAP, 128), 0)
    behind = [jnp.where(slot == 0, 0.0, pltpu.roll(v, 1, 0)) for v in own]
    ahead = [jnp.where(slot == CAP - 1, 0.0, pltpu.roll(v, CAP - 1, 0)) for v in own]
    for a in range(4):
        value = coefficient(table, BASE, a) - coefficient(table, PERF, a) * at_slots
        for b in range(4):
            value = value - coefficient(table, UP + a, b) * behind[b] - coefficient(table, DOWN + a, b) * ahead[b]
        new_state[a * 32:(a + 1) * 32, :] = value


def pack_terms(order, table, state, page):
    terms = sum(coefficient(table, BACK, v) * state[v * 32:(v + 1) * 32, :] for v in range(4))
    high = terms.astype(BF16).astype(F32)
    return pack(high, terms - high, order[...], page)


def spread_block(height, high, low):
    hit = iota((NZ, BLOCK), 0) == height
    return jnp.concatenate([jnp.where(hit, high, 0.0).astype(BF16), jnp.where(hit, low, 0.0).astype(BF16)], axis=0)


def add_blocks(hot, spread):
    return lax.dot_general(hot, spread, (((1,), (1,)), ((), ())), preferred_element_type=F32)


def scatter(heights, hot, order, table, state, spread, parts, page):
    high, low = pack_terms(order, table, state, page)
    parts[0:GROUPS, :], parts[GROUPS:2 * GROUPS, :] = high, low
    for b in range(FEW):
        spread[:, b * BLOCK:(b + 1) * BLOCK] = spread_block(heights[b:b + 1, :], high[b:b + 1, :], low[b:b + 1, :])
    return add_blocks(hot[:, 0:FEW * BLOCK], spread[...])


def scatter_rest(counts, heights, hot, inverse, parts, sums, new_cells):
    sums[...] = jnp.zeros(sums.shape, F32)

    @pl.loop(FEW, blocks_used(counts))
    def _(b):
        block = spread_block(heights[pl.ds(b, 1), :], parts[pl.ds(b, 1), :], parts[pl.ds(b + GROUPS, 1), :])
        sums[...] += add_blocks(hot[:, block_lanes(b)], block)

    new_cells[...] = new_cells[...] - inverse[...] * (sums[:, 0:NZ] + sums[:, NZ:2 * NZ])


def inflow(faces, source, cells, x):
    row, depth = iota((CY, NZ), 0), iota((CY, NZ), 1)
    here, down, up = (pl.ds(p * CY, CY) for p in (x, x - 1, x + 1))
    value = cells[here, :]
    total = source[here, :]
    if x > 0:
        total = total + faces[0, down, :] * cells[down, :]
    if x < CX - 1:
        total = total + faces[1, up, :] * cells[up, :]
    total = total + jnp.where(row == 0, 0.0, pltpu.roll(faces[2, here, :] * value, 1, 0))
    total = total + jnp.where(row == CY - 1, 0.0, pltpu.roll(faces[3, here, :] * value, CY - 1, 0))
    total = total + jnp.where(depth == 0, 0.0, pltpu.roll(faces[4, here, :] * value, 1, 1))
    return total + jnp.where(depth == NZ - 1, 0.0, pltpu.roll(faces[5, here, :] * value, NZ - 1, 1))


def new_planes(wells, faces, inverse, source, cells, new_cells):
    for x in range(CX):
        here = slice(x * CY, (x + 1) * CY)
        new_cells[here, :] = inverse[here, :] * (
            inflow(faces, source, cells, x) - (wells[here, 0:NZ] + wells[here, NZ:2 * NZ]))


def sweep_kernel(counts, heights, order, hot, table, faces, inverse, source, cells, state, new_cells, new_state,
                 turned, spread, picked, page, other_page, parts, sums):
    wells = scatter(heights, hot, order, table, state, spread, parts, page)
    turn(cells, turned)
    pick(heights, hot, turned, picked)
    advance(table, state, unpack(picked, order, other_page), new_state)
    new_planes(wells, faces, inverse, source, cells, new_cells)

    @pl.when(blocks_used(counts) > FEW)
    def _():
        pick_rest(counts, heights, hot, turned, picked)
        more = unpack(picked, order, page)
        for a in range(4):
            here = slice(a * 32, (a + 1) * 32)
            new_state[here, :] = new_state[here, :] - coefficient(table, PERF, a) * more
        scatter_rest(counts, heights, hot, inverse, parts, sums, new_cells)


def first_kernel(far_source, far_inverse, counts, slot_cells, *refs):
    far_out, near_out = refs[:4], refs[4:8]
    columns, heights, order, at_slots = near_out
    source, inverse, hot, turned, picked, page, semaphores = refs[8:]
    copies = bring((far_source, far_inverse), (source, inverse), semaphores)
    order[...] = owner_order(counts)
    pack_slots(slot_cells, order, columns, heights, page)
    make_hot(range(FEW), columns, hot)
    for copy in copies:
        copy.wait()
    source[...] = inverse[...] * source[...]
    turn(source, turned)
    pick(heights, hot, turned, picked)
    at_slots[...] = unpack(picked, order, page)

    @pl.when(blocks_used(counts) > FEW)
    def _():
        make_rest(counts, columns, hot)
        pick_rest(counts, heights, hot, turned, picked)
        at_slots[...] = at_slots[...] + unpack(picked, order, page)

    for copy in bring(near_out, far_out, semaphores):
        copy.wait()


def second_kernel(*refs):
    far, received, (table, hot, source, inverse, faces, counts, heights, order, new_cells, new_state) = (
        refs[:8], refs[8], refs[9:19])
    at_slots, columns, spread, cells, state, page, parts, sums, semaphores = refs[19:]
    copies = bring(far, (columns, counts, at_slots, heights, order, source, inverse, faces), semaphores)
    copies[0].wait()
    make_hot(range(FEW), columns, hot)
    for copy in copies[1:5]:
        copy.wait()
    make_table((BASE, BACK), received, counts, table, state)
    wells = scatter(heights, hot, order, table, state, spread, parts, page)
    make_table([b for b in range(BLOCKS) if b not in (BASE, BACK)], received, counts, table, state)
    advance(table, state, at_slots[...], new_state)
    for copy in copies[5:]:
        copy.wait()
    cells[...] = inverse[...] * source[...]
    new_planes(wells, faces, inverse, source, cells, new_cells)

    @pl.when(blocks_used(counts) > FEW)
    def _():
        make_rest(counts, columns, hot)
        scatter_rest(counts, heights, hot, inverse, parts, sums, new_cells)


def unpack_kernel(received, out):
    out[...] = block_transpose(received[...])


def swap(value, axis, offset):
    count = lax.axis_size(axis)
    pairs = []
    for p in range(offset, count + offset, 2):
        a, b = p % count, (p + 1) % count
        pairs += [(a, b), (b, a)]
    return lax.ppermute(value, axis, pairs)


def all_to_all(rows):
    sent = rows.reshape(128, -1)
    return lax.all_to_all(sent, AXES, split_axis=0, concat_axis=0, tiled=True).reshape(rows.shape)


def exchange(x0, x1, r0, r1):
    return swap(x1, "gx", 1), swap(r1, AXES, 1), swap(x0, "gx", 0), swap(r0, AXES, 0)


def blocks_of(array):
    lead = array.shape[0] if array.ndim == 3 else 1
    return array.reshape(lead, 4, 32, 128).transpose(0, 2, 1, 3).reshape(lead * 128, 128)


def shards(source, cell_inverse, face_coefficients, tile_counts, perf_cells, segment_kinds, segment_inverse,
           upstream_coupling, downstream_coupling, perf_to_segment, segment_to_perf, segment_source):
    source = source.reshape(COLS, NZ)
    inverse = cell_inverse.reshape(COLS, NZ)
    faces = face_coefficients.reshape(6, COLS, NZ)
    slot_cells = perf_cells.reshape(OWNERS, CAP).T
    field, planes = shape(COLS, NZ), shape(128, 128)
    rims = (shape(CY, NZ), shape(CY, NZ), shape(16, NZ), shape(16, NZ))
    turned, spread = pltpu.VMEM((2 * NZ, COLS), BF16), pltpu.VMEM((2 * NZ, FEW * BLOCK), BF16)
    picked, page = pltpu.VMEM((GROUPS, BLOCK), F32), pltpu.VMEM((OWNERS, 128), F32)
    parts, sums = pltpu.VMEM((2 * GROUPS, BLOCK), F32), pltpu.VMEM((COLS, 2 * NZ), F32)
    half = dict(flops=2 * 10**9, moved=8 * 10**6)
    whole = dict(flops=4 * 10**9, moved=16 * 10**6)

    operands = (segment_kinds.reshape(32, 128), blocks_of(segment_inverse), blocks_of(segment_source),
                blocks_of(perf_to_segment), blocks_of(segment_to_perf), blocks_of(upstream_coupling),
                blocks_of(downstream_coupling))
    packed = run(
        fold_kernel, operands, shape(BLOCKS * 128, 128), far=7, limit=56,
        scratch=[pltpu.VMEM((BLOCKS * 128, 128), F32), *(pltpu.VMEM(o.shape, o.dtype) for o in operands),
                 pltpu.SemaphoreType.DMA((7,))])
    received = all_to_all(packed)
    near_field, near_faces = pltpu.VMEM((COLS, NZ), F32), pltpu.VMEM((4, COLS, NZ), F32)
    messages = run(
        start_kernel, (source, inverse, faces), rims, far=3, limit=56,
        scratch=[near_field, near_field, near_faces, near_field, pltpu.SemaphoreType.DMA((6,))])
    messages = exchange(*messages)
    hot_shape = shape(COLS, SLOTS, dtype=BF16)
    slot_shapes = (shape(GROUPS, BLOCK, dtype=jnp.int32), shape(OWNERS, OWNERS, dtype=BF16))
    small = (shape(GROUPS, BLOCK, dtype=jnp.int32), shape(GROUPS, BLOCK, dtype=jnp.int32),
             shape(OWNERS, OWNERS, dtype=BF16), shape(CAP, 128))
    columns, heights, order, at_slots = run(
        first_kernel, (source, inverse, tile_counts, slot_cells), small, far=2, far_out=4, limit=56,
        scratch=[*(pltpu.VMEM(a.shape, a.dtype) for a in small), near_field, near_field,
                 pltpu.VMEM(hot_shape.shape, BF16), turned, picked, page, pltpu.SemaphoreType.DMA((4,))], **half)
    table, hot, source, inverse, faces, counts, heights, order, own_cells, own_state = run(
        second_kernel, (columns, tile_counts, at_slots, heights, order, source, inverse, faces, received),
        (shape(BLOCKS * 128, 128), hot_shape, field, field, shape(6, COLS, NZ), shape(1, OWNERS, dtype=jnp.int32),
         *small[1:3], field, planes), far=8,
        scratch=[pltpu.VMEM((CAP, 128), F32),
                 pltpu.VMEM((GROUPS, BLOCK), jnp.int32), spread, near_field,
                 pltpu.VMEM((128, 128), F32), page, parts, sums, pltpu.SemaphoreType.DMA((8,))], **half)
    for sweep in range(1, ITERS - 1):
        cells, state, *messages = run(
            functools.partial(finish_kernel, sweep == 1),
            (inverse, faces, table, own_cells, own_state, *messages), (field, planes, *rims))
        messages = exchange(*messages)
        own_cells, own_state = run(
            sweep_kernel, (counts, heights, order, hot, table, faces, inverse, source, cells, state), (field, planes),
            scratch=[turned, spread, picked, page, page, parts, sums], **whole)
    cells, packed = run(
        last_kernel, (table, own_state, inverse, own_cells, *messages), (field, planes),
        far_out=1, scratch=[near_field, pltpu.VMEM((128, 128), F32), pltpu.SemaphoreType.DMA((1,))])
    returned = all_to_all(packed)
    states = run(unpack_kernel, (returned,), planes)
    well_adjoint = states.reshape(32, 4, 128).transpose(1, 0, 2).reshape(4, 4096)
    return cells.reshape(CX, CY, NZ), well_adjoint


def solution(mesh):
    in_specs = (
        P("gx", "gy", None),
        P("gx", "gy", None),
        P(None, "gx", "gy", None),
        P(("gx", "gy"), None),
        P(("gx", "gy"), None, None),
        P(("gx", "gy")),
        P(None, None, ("gx", "gy")),
        P(None, None, ("gx", "gy")),
        P(None, None, ("gx", "gy")),
        P(None, ("gx", "gy")),
        P(None, ("gx", "gy")),
        P(None, ("gx", "gy")),
    )
    out_specs = (P("gx", "gy", None), P(None, ("gx", "gy")))
    return jax.shard_map(shards, mesh=mesh, in_specs=in_specs, out_specs=out_specs, check_vma=False)
```

```python
import functools

import jax
import jax.numpy as jnp
from jax import lax
from jax.experimental import pallas as pl
from jax.experimental.pallas import tpu as pltpu
from jax.sharding import PartitionSpec as P

ITERS = 8
F32 = jnp.float32
BF16 = jnp.bfloat16
AXES = ("gx", "gy")
CX, CY, NZ = 8, 64, 256
COLS = CX * CY
CAP, OWNERS = 32, 128
SLOTS = CAP * OWNERS
BLOCK = 8 * CAP
GROUPS = SLOTS // BLOCK
FEW = 9
UP, DOWN, BASE, PERF, BACK, EDGE, BLOCKS = 0, 4, 8, 9, 10, 11, 12
VMEM = pl.BlockSpec(memory_space=pltpu.VMEM)
FAR = pl.BlockSpec(memory_space=pl.ANY)


def run(kernel, operands, out_shape, flops=10**6, moved=10**6, scratch=(), far=0, far_out=0, limit=28):
    many = isinstance(out_shape, (tuple, list))
    operands = [pltpu.with_memory_space_constraint(o, pltpu.HBM) if i < far else o for i, o in enumerate(operands)]
    return pl.pallas_call(
        kernel,
        out_shape=out_shape,
        in_specs=[FAR] * far + [VMEM] * (len(operands) - far),
        out_specs=tuple(FAR if i < far_out else VMEM for i in range(len(out_shape))) if many else VMEM,
        scratch_shapes=list(scratch),
        compiler_params=pltpu.CompilerParams(vmem_limit_bytes=limit * 1024 * 1024),
        cost_estimate=pl.CostEstimate(flops=flops, bytes_accessed=moved, transcendentals=0),
    )(*operands)


def bring(sources, targets, semaphores):
    copies = [pltpu.make_async_copy(a, b, semaphores.at[i]) for i, (a, b) in enumerate(zip(sources, targets))]
    for copy in copies:
        copy.start()
    return copies


def shape(*dims, dtype=F32):
    return jax.ShapeDtypeStruct(dims, dtype)


def iota(dims, axis):
    return lax.broadcasted_iota(jnp.int32, dims, axis)


def block_transpose(x):
    row = iota((128, 128), 0) & 3
    group = iota((128, 128), 1) >> 5
    y = x
    for d in range(1, 4):
        turned = jnp.where(row + d < 4, pltpu.roll(x, 128 - d, 0), pltpu.roll(x, 4 - d, 0))
        y = jnp.where(((group - row) & 3) == d, pltpu.roll(turned, 32 * d, 1), y)
    return y


def before(x):
    turned = pltpu.roll(x, 1, 1)
    return jnp.where(iota(x.shape, 1) == 0, pltpu.roll(turned, 1, 0), turned)


def after(x):
    turned = pltpu.roll(x, 127, 1)
    return jnp.where(iota(x.shape, 1) == 127, pltpu.roll(turned, x.shape[0] - 1, 0), turned)


def fold_kernel(*refs):
    far, out, table, near, semaphores = refs[:7], refs[7], refs[8], refs[9:16], refs[16]
    copies = bring(far, near, semaphores)
    kinds, inverse, base, perf, back, upstream, downstream = near
    for copy in copies[:5]:
        copy.wait()
    valid = (kinds[...] != 0).astype(F32)
    linked = (kinds[...] == 2).astype(F32)

    def plane(ref, a, b):
        return ref[pl.ds(a * 128 + b, 32, stride=4), :]

    def put(block, j, value):
        table[pl.ds(block * 128 + j, 32, stride=4), :] = value

    def finish(blocks):
        for block in blocks:
            out[pl.ds(block, 128, stride=BLOCKS), :] = block_transpose(table[block * 128:(block + 1) * 128, :])

    lane_slot = iota((32, 128), 1) & 31
    for a in range(4):
        row = [plane(inverse, a, c) for c in range(4)]
        start = valid * sum(row[c] * plane(base, 0, c) for c in range(4))
        put(BASE, a, start)
        put(PERF, a, valid * sum(row[c] * plane(perf, 0, c) for c in range(4)))
        put(BACK, a, plane(back, 0, a))
        put(EDGE, a, jnp.where(lane_slot == 0, before(start), after(start)))
    finish((BASE, PERF, BACK, EDGE))
    for block, mask, ref, copy in ((UP, valid * before(linked), upstream, copies[5]),
                                   (DOWN, valid * linked, downstream, copies[6])):
        copy.wait()
        for a in range(4):
            row = [mask * plane(inverse, a, c) for c in range(4)]
            for b in range(4):
                put(block + a, b, sum(row[c] * plane(ref, c, b) for c in range(4)))
        finish(range(block, block + 4))


def owner_order(counts):
    active = (counts[...] > 0).astype(F32)
    earlier = (iota((OWNERS, OWNERS), 0) < iota((OWNERS, OWNERS), 1)).astype(BF16)
    place = jnp.dot(active.astype(BF16), earlier, preferred_element_type=F32).astype(jnp.int32)
    order = jnp.where((iota((OWNERS, OWNERS), 0) == place) & (active > 0.0), 1.0, 0.0)
    return order.astype(BF16)


def pack(high, low, order, page):
    both = jnp.concatenate([high, low], axis=0).astype(BF16)
    packed = lax.dot_general(both, order, (((1,), (1,)), ((), ())), preferred_element_type=F32)
    page[:, 0:2 * CAP] = packed.T
    group = iota((GROUPS, 128), 1) >> 5
    results = []
    for part in range(2):
        halves = []
        for half in range(2):
            total = None
            for g in range(4):
                rows = page[pl.ds(half * 4 + g, GROUPS, stride=8), :]
                shift = (32 * (g - part)) % 128
                rows = pltpu.roll(rows, shift, 1) if shift else rows
                total = rows if total is None else jnp.where(group == g, rows, total)
            halves.append(total)
        results.append(jnp.concatenate(halves, axis=1))
    return results


def unpack(rows, order, page):
    for q in range(8):
        part = rows[:, (q // 4) * 128:(q // 4 + 1) * 128]
        shift = (128 - 32 * (q % 4)) % 128
        page[pl.ds(q, GROUPS, stride=8), :] = pltpu.roll(part, shift, 1) if shift else part
    plane = page[...].T[0:CAP, :]
    high = plane.astype(BF16)
    both = jnp.concatenate([high, (plane - high.astype(F32)).astype(BF16)], axis=0)
    placed = jnp.dot(both, order[...], preferred_element_type=F32)
    return placed[0:CAP] + placed[CAP:2 * CAP]


def pack_slots(slot_cells, order, columns, heights, page):
    column = slot_cells[...] >> 8
    high, low = pack((column & 510).astype(F32), (column & 1).astype(F32), order[...], page)
    columns[...] = (high + low).astype(jnp.int32)
    height = (slot_cells[...] & (NZ - 1)).astype(F32)
    heights[...] = pack(height, jnp.zeros_like(height), order[...], page)[0].astype(jnp.int32)


def make_hot(blocks, columns, hot):
    index = iota((COLS, BLOCK), 0)
    for b in blocks:
        hit = index == columns[b:b + 1, :]
        hot[:, b * BLOCK:(b + 1) * BLOCK] = jnp.where(hit, 1.0, 0.0).astype(BF16)


def blocks_used(counts):
    return (jnp.sum((counts[...] > 0).astype(jnp.int32)) + 7) >> 3


def block_lanes(b):
    return pl.ds(pl.multiple_of(b * BLOCK, BLOCK), BLOCK)


def make_rest(counts, columns, hot):
    @pl.loop(FEW, blocks_used(counts))
    def _(b):
        hit = iota((COLS, BLOCK), 0) == columns[pl.ds(b, 1), :]
        hot[:, block_lanes(b)] = jnp.where(hit, 1.0, 0.0).astype(BF16)


def make_table(blocks, received, counts, table, state):
    for block in blocks:
        part = received[pl.ds(block, 128, stride=BLOCKS), :].T
        if block == PERF:
            part = part * ((iota((128, 128), 0) & 31) < counts[...]).astype(F32)
        if block == BASE:
            state[...] = part
        table[block * 128:(block + 1) * 128, :] = part


def parity_pair(parity, upper, lower):
    even = parity == 0
    return jnp.where(even, upper, lower), jnp.where(even, lower, upper)


def emit(cells, faces, state, x0, x1, r0, r1):
    gx, gy = lax.axis_index("gx"), lax.axis_index("gy")
    last, first = pl.ds(COLS - CY, CY), pl.ds(0, CY)
    x0[...], x1[...] = parity_pair(
        gx & 1, faces[0, last, :] * cells[last, :], faces[1, first, :] * cells[first, :])
    for x in range(CX):
        top, bottom = x * CY + CY - 1, x * CY
        r0[x:x + 1, :], r1[x:x + 1, :] = parity_pair(
            gy & 1, faces[2, top:top + 1, :] * cells[top:top + 1, :],
            faces[3, bottom:bottom + 1, :] * cells[bottom:bottom + 1, :])
    if state is not None:
        for v in range(4):
            r0[8 + v:9 + v, 0:128], r1[8 + v:9 + v, 0:128] = parity_pair(
                gy & 1, state[v * 32 + 31:v * 32 + 32, :], state[v * 32:v * 32 + 1, :])
    else:
        r0[8:16, :] = jnp.zeros((8, NZ), F32)
        r1[8:16, :] = jnp.zeros((8, NZ), F32)


def start_kernel(far_source, far_inverse, far_faces, x0, x1, r0, r1, source, inverse, faces, cells, semaphores):
    top, bottom = pl.ds(COLS - CY, CY), pl.ds(0, CY)
    parts = [(0, top), (1, bottom), (2, pl.ds(0, COLS)), (3, pl.ds(0, COLS))]
    copies = bring(
        [far_source, far_inverse] + [far_faces.at[f, rows, :] for f, rows in parts],
        [source, inverse] + [faces.at[f, rows, :] for f, rows in parts], semaphores)
    for copy in copies[:2]:
        copy.wait()
    cells[...] = inverse[...] * source[...]
    for copy in copies[2:]:
        copy.wait()
    emit(cells, faces, None, x0, x1, r0, r1)


def finish_cells(inverse, cells_in, x0, x1, r0, r1, cells):
    gx, gy = lax.axis_index("gx"), lax.axis_index("gy")
    last_x, last_y = lax.axis_size("gx") - 1, lax.axis_size("gy") - 1
    cells[...] = cells_in[...]
    upper, lower = parity_pair(gx & 1, x0[...], x1[...])
    top, bottom = pl.ds(COLS - CY, CY), pl.ds(0, CY)
    cells[top, :] = cells[top, :] + inverse[top, :] * jnp.where(gx < last_x, upper, 0.0)
    cells[bottom, :] = cells[bottom, :] + inverse[bottom, :] * jnp.where(gx > 0, lower, 0.0)
    upper, lower = parity_pair(gy & 1, r0[0:8, :], r1[0:8, :])
    upper, lower = jnp.where(gy < last_y, upper, 0.0), jnp.where(gy > 0, lower, 0.0)
    for x in range(CX):
        top, bottom = pl.ds(x * CY + CY - 1, 1), pl.ds(x * CY, 1)
        cells[top, :] = cells[top, :] + inverse[top, :] * upper[x:x + 1, :]
        cells[bottom, :] = cells[bottom, :] + inverse[bottom, :] * lower[x:x + 1, :]


def finish_state(first, table, state_in, r0, r1, state):
    gy = lax.axis_index("gy")
    state[...] = state_in[...]
    if first:
        high = [table[EDGE * 128 + v * 32 + 31:EDGE * 128 + v * 32 + 32, :] for v in range(4)]
        low = [table[EDGE * 128 + v * 32:EDGE * 128 + v * 32 + 1, :] for v in range(4)]
    else:
        pairs = [parity_pair(gy & 1, r0[8 + v:9 + v, 0:128], r1[8 + v:9 + v, 0:128]) for v in range(4)]
        high, low = [p[0] for p in pairs], [p[1] for p in pairs]
    for a in range(4):
        k = a * 32
        state[k:k + 1, :] = state[k:k + 1, :] - sum(
            table[(UP + a) * 128 + b * 32:(UP + a) * 128 + b * 32 + 1, :] * low[b] for b in range(4))
        k += 31
        state[k:k + 1, :] = state[k:k + 1, :] - sum(
            table[(DOWN + a) * 128 + b * 32 + 31:(DOWN + a) * 128 + b * 32 + 32, :] * high[b] for b in range(4))


def finish_kernel(first, inverse, faces, table, cells_in, state_in, x1, r1, x0, r0, cells, state, *out):
    finish_state(first, table, state_in, r0, r1, state)
    finish_cells(inverse, cells_in, x0, x1, r0, r1, cells)
    emit(cells, faces, state, *out)


def last_kernel(table, state_in, inverse, cells_in, x1, r1, x0, r0, far_cells, out, cells, state, semaphore):
    finish_cells(inverse, cells_in, x0, x1, r0, r1, cells)
    (copy,) = bring((cells,), (far_cells,), semaphore)
    finish_state(False, table, state_in, r0, r1, state)
    out[...] = state[...].T
    copy.wait()


def turn(cells, turned):
    flipped = cells[...].T
    high = flipped.astype(BF16)
    turned[0:NZ, :] = high
    turned[NZ:2 * NZ, :] = (flipped - high.astype(F32)).astype(BF16)


def pick_block(heights, hot, turned):
    both = jnp.dot(turned[...], hot, preferred_element_type=F32)
    hit = iota((NZ, BLOCK), 0) == heights
    return jnp.sum(jnp.where(hit, both[0:NZ] + both[NZ:2 * NZ], 0.0), axis=0, keepdims=True)


def pick(heights, hot, turned, picked):
    for b in range(FEW):
        picked[b:b + 1, :] = pick_block(heights[b:b + 1, :], hot[:, b * BLOCK:(b + 1) * BLOCK], turned)
    picked[FEW:GROUPS, :] = jnp.zeros((GROUPS - FEW, BLOCK), F32)


def pick_rest(counts, heights, hot, turned, picked):
    picked[...] = jnp.zeros((GROUPS, BLOCK), F32)

    @pl.loop(FEW, blocks_used(counts))
    def _(b):
        picked[pl.ds(b, 1), :] = pick_block(heights[pl.ds(b, 1), :], hot[:, block_lanes(b)], turned)


def coefficient(table, block, j):
    return table[block * 128 + j * 32:block * 128 + (j + 1) * 32, :]


def advance(table, state, at_slots, new_state):
    own = [state[v * 32:(v + 1) * 32, :] for v in range(4)]
    slot = iota((CAP, 128), 0)
    behind = [jnp.where(slot == 0, 0.0, pltpu.roll(v, 1, 0)) for v in own]
    ahead = [jnp.where(slot == CAP - 1, 0.0, pltpu.roll(v, CAP - 1, 0)) for v in own]
    for a in range(4):
        value = coefficient(table, BASE, a) - coefficient(table, PERF, a) * at_slots
        for b in range(4):
            value = value - coefficient(table, UP + a, b) * behind[b] - coefficient(table, DOWN + a, b) * ahead[b]
        new_state[a * 32:(a + 1) * 32, :] = value


def pack_terms(order, table, state, page):
    terms = sum(coefficient(table, BACK, v) * state[v * 32:(v + 1) * 32, :] for v in range(4))
    high = terms.astype(BF16).astype(F32)
    return pack(high, terms - high, order[...], page)


def spread_block(height, high, low):
    hit = iota((NZ, BLOCK), 0) == height
    return jnp.concatenate([jnp.where(hit, high, 0.0).astype(BF16), jnp.where(hit, low, 0.0).astype(BF16)], axis=0)


def add_blocks(hot, spread):
    return lax.dot_general(hot, spread, (((1,), (1,)), ((), ())), preferred_element_type=F32)


def scatter(heights, hot, order, table, state, spread, parts, page):
    high, low = pack_terms(order, table, state, page)
    parts[0:GROUPS, :], parts[GROUPS:2 * GROUPS, :] = high, low
    for b in range(FEW):
        spread[:, b * BLOCK:(b + 1) * BLOCK] = spread_block(heights[b:b + 1, :], high[b:b + 1, :], low[b:b + 1, :])
    return add_blocks(hot[:, 0:FEW * BLOCK], spread[...])


def scatter_rest(counts, heights, hot, inverse, parts, sums, new_cells):
    sums[...] = jnp.zeros(sums.shape, F32)

    @pl.loop(FEW, blocks_used(counts))
    def _(b):
        block = spread_block(heights[pl.ds(b, 1), :], parts[pl.ds(b, 1), :], parts[pl.ds(b + GROUPS, 1), :])
        sums[...] += add_blocks(hot[:, block_lanes(b)], block)

    new_cells[...] = new_cells[...] - inverse[...] * (sums[:, 0:NZ] + sums[:, NZ:2 * NZ])


def inflow(faces, source, cells, x):
    row, depth = iota((CY, NZ), 0), iota((CY, NZ), 1)
    here, down, up = (pl.ds(p * CY, CY) for p in (x, x - 1, x + 1))
    value = cells[here, :]
    total = source[here, :]
    if x > 0:
        total = total + faces[0, down, :] * cells[down, :]
    if x < CX - 1:
        total = total + faces[1, up, :] * cells[up, :]
    total = total + jnp.where(row == 0, 0.0, pltpu.roll(faces[2, here, :] * value, 1, 0))
    total = total + jnp.where(row == CY - 1, 0.0, pltpu.roll(faces[3, here, :] * value, CY - 1, 0))
    total = total + jnp.where(depth == 0, 0.0, pltpu.roll(faces[4, here, :] * value, 1, 1))
    return total + jnp.where(depth == NZ - 1, 0.0, pltpu.roll(faces[5, here, :] * value, NZ - 1, 1))


def new_planes(wells, faces, inverse, source, cells, new_cells):
    for x in range(CX):
        here = slice(x * CY, (x + 1) * CY)
        new_cells[here, :] = inverse[here, :] * (
            inflow(faces, source, cells, x) - (wells[here, 0:NZ] + wells[here, NZ:2 * NZ]))


def sweep_kernel(counts, heights, order, hot, table, faces, inverse, source, cells, state, new_cells, new_state,
                 turned, spread, picked, page, other_page, parts, sums):
    wells = scatter(heights, hot, order, table, state, spread, parts, page)
    turn(cells, turned)
    pick(heights, hot, turned, picked)
    advance(table, state, unpack(picked, order, other_page), new_state)
    new_planes(wells, faces, inverse, source, cells, new_cells)

    @pl.when(blocks_used(counts) > FEW)
    def _():
        pick_rest(counts, heights, hot, turned, picked)
        more = unpack(picked, order, page)
        for a in range(4):
            here = slice(a * 32, (a + 1) * 32)
            new_state[here, :] = new_state[here, :] - coefficient(table, PERF, a) * more
        scatter_rest(counts, heights, hot, inverse, parts, sums, new_cells)


def first_kernel(far_source, far_inverse, counts, slot_cells, *refs):
    far_out, near_out = refs[:4], refs[4:8]
    columns, heights, order, at_slots = near_out
    source, inverse, hot, turned, picked, page, semaphores = refs[8:]
    copies = bring((far_source, far_inverse), (source, inverse), semaphores)
    order[...] = owner_order(counts)
    pack_slots(slot_cells, order, columns, heights, page)
    make_hot(range(FEW), columns, hot)
    for copy in copies:
        copy.wait()
    source[...] = inverse[...] * source[...]
    turn(source, turned)
    pick(heights, hot, turned, picked)
    at_slots[...] = unpack(picked, order, page)

    @pl.when(blocks_used(counts) > FEW)
    def _():
        make_rest(counts, columns, hot)
        pick_rest(counts, heights, hot, turned, picked)
        at_slots[...] = at_slots[...] + unpack(picked, order, page)

    for copy in bring(near_out, far_out, semaphores):
        copy.wait()


def second_kernel(*refs):
    far, received, (table, hot, source, inverse, faces, counts, heights, order, new_cells, new_state) = (
        refs[:8], refs[8], refs[9:19])
    at_slots, columns, spread, cells, state, page, parts, sums, semaphores = refs[19:]
    copies = bring(far, (columns, counts, at_slots, heights, order, source, inverse, faces), semaphores)
    make_table([b for b in range(BLOCKS) if b != PERF], received, counts, table, state)
    copies[0].wait()
    make_hot(range(FEW), columns, hot)
    for copy in copies[1:5]:
        copy.wait()
    wells = scatter(heights, hot, order, table, state, spread, parts, page)
    make_table((PERF,), received, counts, table, state)
    advance(table, state, at_slots[...], new_state)
    for copy in copies[5:]:
        copy.wait()
    cells[...] = inverse[...] * source[...]
    new_planes(wells, faces, inverse, source, cells, new_cells)

    @pl.when(blocks_used(counts) > FEW)
    def _():
        make_rest(counts, columns, hot)
        scatter_rest(counts, heights, hot, inverse, parts, sums, new_cells)


def unpack_kernel(received, out):
    out[...] = block_transpose(received[...])


def swap(value, axis, offset):
    count = lax.axis_size(axis)
    pairs = []
    for p in range(offset, count + offset, 2):
        a, b = p % count, (p + 1) % count
        pairs += [(a, b), (b, a)]
    return lax.ppermute(value, axis, pairs)


def all_to_all(rows):
    sent = rows.reshape(128, -1)
    return lax.all_to_all(sent, AXES, split_axis=0, concat_axis=0, tiled=True).reshape(rows.shape)


def exchange(x0, x1, r0, r1):
    return swap(x1, "gx", 1), swap(r1, AXES, 1), swap(x0, "gx", 0), swap(r0, AXES, 0)


def blocks_of(array):
    lead = array.shape[0] if array.ndim == 3 else 1
    return array.reshape(lead, 4, 32, 128).transpose(0, 2, 1, 3).reshape(lead * 128, 128)


def shards(source, cell_inverse, face_coefficients, tile_counts, perf_cells, segment_kinds, segment_inverse,
           upstream_coupling, downstream_coupling, perf_to_segment, segment_to_perf, segment_source):
    source = source.reshape(COLS, NZ)
    inverse = cell_inverse.reshape(COLS, NZ)
    faces = face_coefficients.reshape(6, COLS, NZ)
    slot_cells = perf_cells.reshape(OWNERS, CAP).T
    field, planes = shape(COLS, NZ), shape(128, 128)
    rims = (shape(CY, NZ), shape(CY, NZ), shape(16, NZ), shape(16, NZ))
    turned, spread = pltpu.VMEM((2 * NZ, COLS), BF16), pltpu.VMEM((2 * NZ, FEW * BLOCK), BF16)
    picked, page = pltpu.VMEM((GROUPS, BLOCK), F32), pltpu.VMEM((OWNERS, 128), F32)
    parts, sums = pltpu.VMEM((2 * GROUPS, BLOCK), F32), pltpu.VMEM((COLS, 2 * NZ), F32)
    half = dict(flops=2 * 10**9, moved=8 * 10**6)
    whole = dict(flops=4 * 10**9, moved=16 * 10**6)

    operands = (segment_kinds.reshape(32, 128), blocks_of(segment_inverse), blocks_of(segment_source),
                blocks_of(perf_to_segment), blocks_of(segment_to_perf), blocks_of(upstream_coupling),
                blocks_of(downstream_coupling))
    packed = run(
        fold_kernel, operands, shape(BLOCKS * 128, 128), far=7, limit=56,
        scratch=[pltpu.VMEM((BLOCKS * 128, 128), F32), *(pltpu.VMEM(o.shape, o.dtype) for o in operands),
                 pltpu.SemaphoreType.DMA((7,))])
    received = all_to_all(packed)
    near_field, near_faces = pltpu.VMEM((COLS, NZ), F32), pltpu.VMEM((4, COLS, NZ), F32)
    messages = run(
        start_kernel, (source, inverse, faces), rims, far=3, limit=56,
        scratch=[near_field, near_field, near_faces, near_field, pltpu.SemaphoreType.DMA((6,))])
    messages = exchange(*messages)
    hot_shape = shape(COLS, SLOTS, dtype=BF16)
    slot_shapes = (shape(GROUPS, BLOCK, dtype=jnp.int32), shape(OWNERS, OWNERS, dtype=BF16))
    small = (shape(GROUPS, BLOCK, dtype=jnp.int32), shape(GROUPS, BLOCK, dtype=jnp.int32),
             shape(OWNERS, OWNERS, dtype=BF16), shape(CAP, 128))
    columns, heights, order, at_slots = run(
        first_kernel, (source, inverse, tile_counts, slot_cells), small, far=2, far_out=4, limit=56,
        scratch=[*(pltpu.VMEM(a.shape, a.dtype) for a in small), near_field, near_field,
                 pltpu.VMEM(hot_shape.shape, BF16), turned, picked, page, pltpu.SemaphoreType.DMA((4,))], **half)
    table, hot, source, inverse, faces, counts, heights, order, own_cells, own_state = run(
        second_kernel, (columns, tile_counts, at_slots, heights, order, source, inverse, faces, received),
        (shape(BLOCKS * 128, 128), hot_shape, field, field, shape(6, COLS, NZ), shape(1, OWNERS, dtype=jnp.int32),
         *small[1:3], field, planes), far=8,
        scratch=[pltpu.VMEM((CAP, 128), F32),
                 pltpu.VMEM((GROUPS, BLOCK), jnp.int32), spread, near_field,
                 pltpu.VMEM((128, 128), F32), page, parts, sums, pltpu.SemaphoreType.DMA((8,))], **half)
    for sweep in range(1, ITERS - 1):
        cells, state, *messages = run(
            functools.partial(finish_kernel, sweep == 1),
            (inverse, faces, table, own_cells, own_state, *messages), (field, planes, *rims))
        messages = exchange(*messages)
        own_cells, own_state = run(
            sweep_kernel, (counts, heights, order, hot, table, faces, inverse, source, cells, state), (field, planes),
            scratch=[turned, spread, picked, page, page, parts, sums], **whole)
    cells, packed = run(
        last_kernel, (table, own_state, inverse, own_cells, *messages), (field, planes),
        far_out=1, scratch=[near_field, pltpu.VMEM((128, 128), F32), pltpu.SemaphoreType.DMA((1,))])
    returned = all_to_all(packed)
    states = run(unpack_kernel, (returned,), planes)
    well_adjoint = states.reshape(32, 4, 128).transpose(1, 0, 2).reshape(4, 4096)
    return cells.reshape(CX, CY, NZ), well_adjoint


def solution(mesh):
    in_specs = (
        P("gx", "gy", None),
        P("gx", "gy", None),
        P(None, "gx", "gy", None),
        P(("gx", "gy"), None),
        P(("gx", "gy"), None, None),
        P(("gx", "gy")),
        P(None, None, ("gx", "gy")),
        P(None, None, ("gx", "gy")),
        P(None, None, ("gx", "gy")),
        P(None, ("gx", "gy")),
        P(None, ("gx", "gy")),
        P(None, ("gx", "gy")),
    )
    out_specs = (P("gx", "gy", None), P(None, ("gx", "gy")))
    return jax.shard_map(shards, mesh=mesh, in_specs=in_specs, out_specs=out_specs, check_vma=False)
```
